1024 devices in a mesh: blk: 16 (over y_hi, x, core), bal: 64 (over z, y_lo).
Axes of the slice: x: 4, y: 4 (y_hi: 2, y_lo: 2; y = y_hi * 2 + y_lo), z: 32, core: 2. Of those that a mesh axis runs over, the one named last changes fastest.
Arguments:
- patch_keys: bfloat16 [393216, 1536], P(('blk', 'bal')), may hold values from -128 to 128
- patch_values: bfloat16 [393216, 1536], P(('blk', 'bal')), may hold values from -6 to 6
- lengths: int32 [1024, 3], P(('blk', 'bal')), may hold values from 1 to 256, 384 in all within a row
- probe_query: bfloat16 [1536], replicated, may hold values from -3 to 3
- projection: bfloat16 [1536, 1152], replicated, may hold values from -0.15625 to 0.15625
- text_embeds: bfloat16 [3072, 1152], P(('blk', 'bal')), may hold values from -2 to 2
- pair_group: int32 [3072], replicated, may hold values from 0 to 3071
- logit_scale: float32 [1], replicated, may hold values from 10 to 30
- logit_bias: float32 [1], replicated, may hold values from -2 to 0
Outputs:
- pooled_grad: float32 [3072, 1536], P(('blk', 'bal'))
- text_grad: float32 [3072, 1152], P(('blk', 'bal'))
The draws below stay inside these ranges and needn't reach their ends.
Inputs may be any that keep to these rules, and one draw needn't show every extreme that they name: `lengths`: the 3 counts of a device fill its 384 rows; some image has 256 patches. `pair_group`: pairs with equal groups are positive.
All inputs are finite; a program needn't handle non-finite values.
Results may differ from the reference program's by a relative error of at most 0.0065.
Values may be sent and summed in bfloat16 or wider, within the bound.
No kernel may reach another device: no remote copies, remote signals or barrier semaphores. Data moves between devices by JAX's collectives and lax.ppermute only.
A program may use at most 32 MiB of HBM per device.

```python
import math
import jax
import jax.numpy as jnp
import numpy as np
from jax import lax

D = 1536
H = 16
HD = 96
E = 1152
IMG_DEV = 3
MOST = 256
ROWS_DEV = 384
PAIRS = 3072
ROWS = 393216
N_BLK = 16
N_BAL = 64


def probe_base(key):
    return jnp.clip(jax.random.normal(key, (D,), jnp.float32), -3.0, 3.0)


def draw_probe_query(key, part):
    base = probe_base(key)
    return base.astype(jnp.bfloat16)


def draw_patch_keys(key, part):
    key = jax.random.fold_in(key, 5)
    noise = jnp.clip(jax.random.normal(key, (ROWS, D), jnp.float32), -6.0, 6.0)
    return noise.astype(jnp.bfloat16)


def draw_text_embeds(key, part):
    key = jax.random.fold_in(key, 7)
    first, second, third = jax.random.split(key, 3)
    row_scale = jnp.exp(jax.random.uniform(second, (PAIRS, 1), jnp.float32, jnp.log(0.3), jnp.log(3.0)))
    col_scale = jnp.exp(jax.random.uniform(third, (1, E), jnp.float32, 0.0, jnp.log(10.0))) / 4.0
    noise = jnp.clip(jax.random.normal(first, (PAIRS, E), jnp.float32), -6.0, 6.0)
    values = noise * row_scale * col_scale / jnp.sqrt(1.0 * E)
    return jnp.clip(values, -2.0, 2.0).astype(jnp.bfloat16)


def with_ends(values, key, smallest, high):
    spot = [jax.random.randint(jax.random.fold_in(key, axis), (), 0, length) for axis, length in enumerate(values.shape)]
    longest = values.shape.index(max(values.shape))
    next_to = spot[:longest] + [(spot[longest] + 1) % values.shape[longest]] + spot[longest + 1:]
    return values.at[tuple(spot)].set(smallest).at[tuple(next_to)].set(high)


def shard_levels(own_key, extent, shards, low, top_value):
    loudness = 1.0
    for position, shards_of in shards:
        heights = jax.random.uniform(jax.random.fold_in(jax.random.fold_in(own_key, 6), position), (shards_of,), jnp.float32, low / len(shards), top_value / len(shards))
        loudness = loudness * jnp.repeat(jnp.exp(heights), extent[position] // shards_of).reshape((-1,) + (1,) * (len(extent) - 1 - position))
    return loudness


def split_up(count, total, reach, slope):
    portions = [(1 << 20) // math.isqrt(standing ** slope) + 1 for standing in range(2, count + 1)]
    spare, holding = total - reach - (count - 1), [1] * (count - 1)
    while spare > 0:
        movable = [i for i in range(count - 1) if holding[i] < reach]
        pool, budget = sum([portions[i] for i in movable]), spare
        for i in movable:
            extra = min(reach - holding[i], max(1, budget * portions[i] // pool), spare)
            holding[i] = holding[i] + extra
            spare = spare - extra
    return np.array([reach] + holding)


def ragged_sizes(rng, amount, total, bound, slope):
    if amount == 2:
        one = jax.random.randint(rng, (), max(1, total - bound), min(bound, total - 1) + 1)
        return jnp.stack([one, total - one])
    sizes = jnp.asarray(split_up(amount, total, bound, slope), jnp.int32)
    twos = (amount - 1) // 2
    source_of, receiver = sizes[1:1 + 2 * twos:2], sizes[2:2 + 2 * twos:2]
    room = jnp.minimum(source_of - 1, bound - receiver)
    shifted = jax.random.randint(jax.random.fold_in(rng, 1), (twos,), 0, 1 << 20) % (room + 1)
    sizes = sizes.at[1:1 + 2 * twos:2].set(source_of - shifted).at[2:2 + 2 * twos:2].set(receiver + shifted)
    return sizes[jax.random.permutation(jax.random.fold_in(rng, 2), amount)]


def normal_values(stream_key, shape, spread, most, cuts=(), kind=jnp.bfloat16):
    gain = shard_levels(stream_key, shape, cuts, -0.22, 0.18) if cuts else 1.0
    result = jax.random.normal(stream_key, shape, jnp.float32) * spread * gain
    return jnp.minimum(jnp.maximum(result, -most), most).astype(kind)


def setup_inputs(seed: int = 0) -> dict:
    arg_keys = jax.random.split(jax.random.key(seed), 10)
    patch_keys = draw_patch_keys(jax.random.fold_in(arg_keys[9], 71), 0)
    patch_values = normal_values(arg_keys[1], (ROWS, D), 1.0, 6.0, ((0, 1024),))
    lengths = jax.vmap(lambda own: ragged_sizes(own, IMG_DEV, ROWS_DEV, MOST, 2))(jax.random.split(arg_keys[2], (N_BLK * N_BAL))).reshape((N_BLK * N_BAL, IMG_DEV)).astype(jnp.int32)
    probe_query = draw_probe_query(jax.random.fold_in(arg_keys[9], 71), 0)
    projection = normal_values(arg_keys[4], (D, E), D ** -0.5, 0.15625)
    text_embeds = draw_text_embeds(jax.random.fold_in(arg_keys[9], 71), 0)
    pair_group = with_ends(jax.random.randint(arg_keys[6], (PAIRS,), 0, PAIRS), jax.random.fold_in(arg_keys[6], 1), 0, PAIRS - 1).astype(jnp.int32)
    logit_scale = jnp.clip(jnp.exp(jax.random.uniform(arg_keys[7], (1,), jnp.float32, math.log(10.0), math.log(30.0))), 10.0, 30.0)
    logit_bias = jnp.clip(jax.random.uniform(arg_keys[8], (1,), jnp.float32, -2.0, 0.0), -2.0, 0.0)
    return {"patch_keys": patch_keys, "patch_values": patch_values, "lengths": lengths, "probe_query": probe_query, "projection": projection, "text_embeds": text_embeds, "pair_group": pair_group, "logit_scale": logit_scale, "logit_bias": logit_bias}


epsilon = 1e-06

def pool_block(key_rows, value_rows, img_lengths, probe_query):
    total_rows = key_rows.shape[0]
    scores = jnp.einsum('rhc,hc->rh', key_rows.astype(jnp.float32).reshape(total_rows, H, HD), probe_query.astype(jnp.float32).reshape(H, HD)) / math.sqrt(HD)
    ending = jnp.cumsum(img_lengths).astype(jnp.int32)
    starts = (ending - img_lengths).astype(jnp.int32)
    row_index = jnp.arange(total_rows, dtype=jnp.int32)
    member = (row_index[None, :] >= starts[:, None]) & (row_index[None, :] < ending[:, None])
    masked = jnp.where(member[:, :, None], scores[None, :, :], -jnp.inf)
    peak_score = lax.optimization_barrier(jnp.max(masked, axis=1, keepdims=True))
    exp_terms = jnp.where(member[:, :, None], jnp.exp(masked - peak_score), 0.0)
    weights = (exp_terms / lax.optimization_barrier(jnp.sum(exp_terms, axis=1, keepdims=True))).astype(jnp.bfloat16)
    pooled = jnp.einsum('krh,rhc->khc', weights.astype(jnp.float32), value_rows.astype(jnp.float32).reshape(total_rows, H, HD))
    return pooled.reshape(img_lengths.shape[0], H * HD).astype(jnp.bfloat16)

def reference(patch_keys, patch_values, lengths, probe_query, projection, text_embeds, pair_group, logit_scale, logit_bias):
    device_count = lengths.shape[0]
    key_blocks = patch_keys.reshape(device_count, -1, patch_keys.shape[1])
    value_blocks = patch_values.reshape(device_count, -1, patch_values.shape[1])
    pooled = lax.map(lambda device_item: pool_block(device_item[0], device_item[1], device_item[2], probe_query), (key_blocks, value_blocks, lengths))
    pooled = pooled.reshape(-1, D)
    projected = jnp.dot(pooled, projection, preferred_element_type=jnp.float32)
    proj_norm = jnp.sqrt(lax.optimization_barrier(jnp.sum(projected * projected, axis=1, keepdims=True)) + epsilon)
    img_unit = (projected / proj_norm).astype(jnp.bfloat16)
    text_wide = text_embeds.astype(jnp.float32)
    text_norm = jnp.sqrt(lax.optimization_barrier(jnp.sum(text_wide * text_wide, axis=1, keepdims=True)) + epsilon)
    txt_unit = (text_wide / text_norm).astype(jnp.bfloat16)
    logit_mult = logit_scale[0]
    shift_val = logit_bias[0]
    block_rows = IMG_DEV * N_BAL
    img_blocks = img_unit.reshape(-1, block_rows, E)
    id_blocks = pair_group.reshape(-1, block_rows)

    def tile_step(text_acc, block_item):
        img_rows, block_ids = block_item
        logits = jnp.dot(img_rows, txt_unit.T, preferred_element_type=jnp.float32) * logit_mult + shift_val
        labels = jnp.where(block_ids[:, None] == pair_group[None, :], 1.0, -1.0).astype(jnp.float32)
        coeffs = (-labels * jax.nn.sigmoid(-labels * logits) * logit_mult).astype(jnp.bfloat16)
        d_rows = jnp.dot(coeffs, txt_unit, preferred_element_type=jnp.float32)
        text_acc = text_acc + jnp.dot(coeffs.T, img_rows, preferred_element_type=jnp.float32)
        return (text_acc, d_rows)
    d_txt, d_img = lax.scan(tile_step, jnp.zeros((pair_group.shape[0], E), jnp.float32), (img_blocks, id_blocks))
    d_img = d_img.reshape(-1, E)
    proj_dir = projected / proj_norm
    d_proj = ((d_img - lax.optimization_barrier(jnp.sum(d_img * proj_dir, axis=1, keepdims=True)) * proj_dir) / proj_norm).astype(jnp.bfloat16)
    pooled_grad = jnp.dot(d_proj, projection.T, preferred_element_type=jnp.float32)
    text_dir = text_wide / text_norm
    text_grad = (d_txt - lax.optimization_barrier(jnp.sum(d_txt * text_dir, axis=1, keepdims=True)) * text_dir) / text_norm
    return (pooled_grad, text_grad)
```

```python
import math

import jax
import jax.numpy as jnp
from jax import lax
from jax.sharding import Mesh, PartitionSpec as P

H = 16
HD = 96

AXES = ("y_hi", "x", "core", "z", "y_lo")
SIZES = (2, 4, 2, 32, 2)
PLANE = ("core", "y_hi", "y_lo", "x")
AXES_PLANE = ("y_hi", "x", "core", "y_lo")

epsilon = 1e-06


def pool_device(key_rows, value_rows, img_lengths, probe_query):
    total_rows = key_rows.shape[0]
    scores = jnp.einsum(
        "rhc,hc->rh",
        key_rows.reshape(total_rows, H, HD),
        probe_query.reshape(H, HD),
        preferred_element_type=jnp.float32,
    ) / math.sqrt(HD)
    ending = jnp.cumsum(img_lengths)
    starts = ending - img_lengths
    row_index = jnp.arange(total_rows, dtype=jnp.int32)
    member = (row_index[None, :] >= starts[:, None]) & (row_index[None, :] < ending[:, None])
    masked = jnp.where(member[:, :, None], scores[None, :, :], -jnp.inf)
    peak_score = jnp.max(masked, axis=1, keepdims=True)
    exp_terms = jnp.where(member[:, :, None], jnp.exp(masked - peak_score), 0.0)
    weights = (exp_terms / jnp.sum(exp_terms, axis=1, keepdims=True)).astype(jnp.bfloat16)
    pooled = jnp.einsum(
        "krh,rhc->khc",
        weights,
        value_rows.reshape(total_rows, H, HD),
        preferred_element_type=jnp.float32,
    )
    return pooled.reshape(img_lengths.shape[0], H * HD).astype(jnp.bfloat16)


def shards(
    patch_keys,
    patch_values,
    lengths,
    probe_query,
    projection,
    text_embeds,
    pair_group,
    logit_scale,
    logit_bias,
):
    count, width = text_embeds.shape
    sizes = tuple(lax.axis_size(axis) for axis in AXES)
    n_z = lax.axis_size("z")
    n_plane = lax.axis_size(PLANE)
    lanes = 128
    packed = (2 * count * width // lanes, lanes)
    text_wide = text_embeds.astype(jnp.float32)
    text_norm = jnp.sqrt(jnp.sum(text_wide * text_wide, axis=1, keepdims=True) + epsilon)
    txt_unit = (text_wide / text_norm).astype(jnp.bfloat16)

    pooled = pool_device(patch_keys, patch_values, lengths[0], probe_query)
    projected = jnp.dot(pooled, projection, preferred_element_type=jnp.float32)
    proj_norm = jnp.sqrt(jnp.sum(projected * projected, axis=1, keepdims=True) + epsilon)
    img_unit = (projected / proj_norm).astype(jnp.bfloat16)

    block = jnp.concatenate([img_unit, txt_unit]).reshape(packed)
    line = lax.all_to_all(jnp.broadcast_to(block, (n_z,) + packed), "z", 0, 0, tiled=True)
    plane = block[None]
    for axis in PLANE[::-1]:
        plane = lax.all_gather(plane, axis, axis=0, tiled=True)
    line = line.reshape(-1, width)
    plane = plane.reshape(-1, width)

    place = dict((axis, lax.axis_index(axis)) for axis in AXES)
    ids = pair_group.reshape(sizes + (count,))
    at_z = lax.dynamic_index_in_dim(ids, place["z"], 3, keepdims=False)
    plane_ids = jnp.transpose(at_z, [AXES_PLANE.index(axis) for axis in PLANE] + [4]).reshape(n_plane, 1, count)
    line_ids = lax.dynamic_slice(
        ids,
        [0 if axis == "z" else place[axis] for axis in AXES] + [0],
        [n_z if axis == "z" else 1 for axis in AXES] + [count],
    ).reshape(n_z, 1, count)
    plane_ids = jnp.broadcast_to(plane_ids, (n_plane, 2, count)).reshape(-1)
    line_ids = jnp.broadcast_to(line_ids, (n_z, 2, count)).reshape(-1)
    plane_kind = jnp.arange(n_plane * 2 * count, dtype=jnp.int32) // count % 2
    line_kind = jnp.arange(n_z * 2 * count, dtype=jnp.int32) // count % 2

    logits = (
        jnp.einsum("pe,le->pl", plane, line, preferred_element_type=jnp.float32) * logit_scale[0]
        + logit_bias[0]
    )
    labels = jnp.where(plane_ids[:, None] == line_ids[None, :], jnp.float32(1.0), jnp.float32(-1.0))
    coeffs = -labels * jax.nn.sigmoid(-labels * logits) * logit_scale[0]
    coeffs = jnp.where(plane_kind[:, None] != line_kind[None, :], coeffs, 0.0).astype(jnp.bfloat16)
    parts = jnp.einsum("pl,le->pe", coeffs, line, preferred_element_type=jnp.float32)
    parts = parts.astype(jnp.bfloat16).reshape((n_plane,) + packed)
    parts = lax.all_to_all(parts, PLANE, 0, 0, tiled=True)
    d_units = jnp.sum(parts.astype(jnp.float32), axis=0).reshape(2 * count, width)
    d_img, d_txt = d_units[:count], d_units[count:]

    proj_dir = projected / proj_norm
    d_proj = (
        (d_img - jnp.sum(d_img * proj_dir, axis=1, keepdims=True) * proj_dir) / proj_norm
    ).astype(jnp.bfloat16)
    pooled_grad = jnp.dot(d_proj, projection.T, preferred_element_type=jnp.float32)
    text_dir = text_wide / text_norm
    text_grad = (d_txt - jnp.sum(d_txt * text_dir, axis=1, keepdims=True) * text_dir) / text_norm
    return (pooled_grad, text_grad)


def solution(mesh):
    fine = Mesh(mesh.devices.reshape(SIZES), AXES)
    rows = P(AXES, None)
    in_specs = (rows, rows, rows, P(), P(), rows, P(), P(), P())
    return jax.shard_map(
        shards, mesh=fine, in_specs=in_specs, out_specs=(rows, rows), check_vma=False
    )
```

```python
import math

import jax
import jax.numpy as jnp
from jax import lax
from jax.experimental import pallas as pl
from jax.experimental.pallas import tpu as pltpu
from jax.sharding import Mesh, PartitionSpec as P

H = 16
HD = 96

AXES = ("y_hi", "x", "core", "z", "y_lo")
SIZES = (2, 4, 2, 32, 2)
PLANE = ("y_hi", "x", "core", "y_lo")

BLOCK = 8
HALF = 4

epsilon = 1e-06
VMEM = pl.BlockSpec(memory_space=pltpu.VMEM)
SMEM = pl.BlockSpec(memory_space=pltpu.SMEM)
PARAMS = pltpu.CompilerParams(vmem_limit_bytes=24 << 20)


def row_norm(rows):
    return jnp.sqrt(jnp.sum(rows * rows, axis=1, keepdims=True) + epsilon)


def units_kernel(
    lengths, keys, values, probe, projection, text, block, projected, pooled, units
):
    n_rows, width = keys.shape
    head = lax.broadcasted_iota(jnp.int32, (H, width), 0)
    own = lax.broadcasted_iota(jnp.int32, (H, width), 1) // HD == head
    query = jnp.where(own, probe[...].astype(jnp.float32), 0.0).astype(jnp.bfloat16)
    scores = lax.dot_general(
        query, keys[...], (((1,), (1,)), ((), ())), preferred_element_type=jnp.float32
    ) / math.sqrt(HD)
    row = lax.broadcasted_iota(jnp.int32, (H, n_rows), 1)
    start = jnp.int32(0)
    weights = []
    for image in range(lengths.shape[1]):
        end = start + lengths[0, image]
        member = (row >= start) & (row < end)
        masked = jnp.where(member, scores, -jnp.inf)
        terms = jnp.exp(masked - jnp.max(masked, axis=1, keepdims=True))
        weights.append((terms / jnp.sum(terms, axis=1, keepdims=True)).astype(jnp.bfloat16))
        start = end
    mixed = jnp.dot(
        jnp.concatenate(weights), values[...], preferred_element_type=jnp.float32
    )
    pooled[...] = jnp.zeros_like(pooled)
    for image in range(lengths.shape[1]):
        part = mixed[image * H : (image + 1) * H]
        pooled[image : image + 1, :] = jnp.sum(jnp.where(own, part, 0.0), axis=0, keepdims=True)
    proj = jnp.dot(
        pooled[...].astype(jnp.bfloat16), projection[...], preferred_element_type=jnp.float32
    )[:BLOCK]
    projected[...] = proj
    units[...] = proj / row_norm(proj)
    text_wide = text[...].astype(jnp.float32)
    count = text.shape[0]
    units[HALF : HALF + count, :] = text_wide / row_norm(text_wide)
    filled = lax.broadcasted_iota(jnp.int32, units.shape, 0) % HALF < count
    block[...] = jnp.where(filled, units[...], 0.0).astype(jnp.bfloat16)


def pick(groups, positions, axis):
    n_rows, lanes = groups.shape
    n = positions.shape[axis]
    high, low = groups // 64, groups % 64
    pieces = []
    for digit in (high, low):
        digit = digit.astype(jnp.float32).astype(jnp.bfloat16)
        if axis == 0:
            lane = lax.broadcasted_iota(jnp.int32, (n, lanes), 1)
            hot = jnp.where(lane == positions % lanes, 1.0, 0.0).astype(jnp.bfloat16)
            found = lax.dot_general(
                hot, digit, (((1,), (1,)), ((), ())), preferred_element_type=jnp.float32
            )
            line = lax.broadcasted_iota(jnp.int32, (n, n_rows), 1)
        else:
            lane = lax.broadcasted_iota(jnp.int32, (lanes, n), 0)
            hot = jnp.where(lane == positions % lanes, 1.0, 0.0).astype(jnp.bfloat16)
            found = jnp.dot(digit, hot, preferred_element_type=jnp.float32)
            line = lax.broadcasted_iota(jnp.int32, (n_rows, n), 0)
        kept = jnp.where(line == positions // lanes, found, 0.0)
        pieces.append(jnp.sum(kept, axis=1 - axis, keepdims=True))
    return pieces[0] * 64.0 + pieces[1]


def tile_kernel(count, plane, line, groups, scale, bias, parts):
    n_x, n_core, n_z, n_y = (lax.axis_size(axis) for axis in ("x", "core", "z", "y_lo"))
    blk = (lax.axis_index("y_hi") * n_x + lax.axis_index("x")) * n_core + lax.axis_index("core")
    per_blk = n_z * n_y * count
    at = lax.broadcasted_iota(jnp.int32, (plane.shape[0], 1), 0)
    member, slot = at // BLOCK, jnp.minimum(at % HALF, count - 1)
    plane_at = (
        member // n_y * per_blk
        + (lax.axis_index("z") * n_y + member % n_y) * count
        + slot
    )
    plane_kind = at % BLOCK // HALF
    at = lax.broadcasted_iota(jnp.int32, (1, line.shape[0]), 1)
    member, slot = at // BLOCK, jnp.minimum(at % HALF, count - 1)
    line_at = blk * per_blk + (member * n_y + lax.axis_index("y_lo")) * count + slot
    line_kind = at % BLOCK // HALF
    plane_ids = pick(groups[...], plane_at, 0)
    line_ids = pick(groups[...], line_at, 1)

    logits = (
        lax.dot_general(
            plane[...], line[...], (((1,), (1,)), ((), ())), preferred_element_type=jnp.float32
        )
        * scale[0]
        + bias[0]
    )
    labels = jnp.where(plane_ids == line_ids, 1.0, -1.0)
    coeffs = -labels * jax.nn.sigmoid(-labels * logits) * scale[0]
    coeffs = jnp.where(plane_kind != line_kind, coeffs, 0.0).astype(jnp.bfloat16)
    parts[...] = jnp.dot(coeffs, line[...], preferred_element_type=jnp.float32).astype(jnp.bfloat16)


def grads_kernel(parts, projected, projection, text, pooled_grad, text_grad, sums):
    count, width = text.shape
    total = parts[...].astype(jnp.float32).reshape(-1, BLOCK, width)
    total = jnp.sum(total, axis=0)
    sums[...] = total
    proj = projected[...]
    norm = row_norm(proj)
    u = proj / norm
    d_proj = (total - jnp.sum(total * u, axis=1, keepdims=True) * u) / norm
    d_proj = jnp.concatenate([d_proj, jnp.zeros_like(d_proj)]).astype(jnp.bfloat16)
    pooled_grad[...] = lax.dot_general(
        d_proj, projection[...], (((1,), (1,)), ((), ())), preferred_element_type=jnp.float32
    )[:count]
    text_wide = text[...].astype(jnp.float32)
    norm = row_norm(text_wide)
    v = text_wide / norm
    d_txt = sums[HALF : HALF + count, :]
    text_grad[...] = (d_txt - jnp.sum(d_txt * v, axis=1, keepdims=True) * v) / norm


def shards(
    patch_keys,
    patch_values,
    lengths,
    probe_query,
    projection,
    text_embeds,
    pair_group,
    logit_scale,
    logit_bias,
):
    count, width = text_embeds.shape
    depth = patch_keys.shape[1]
    n_z = lax.axis_size("z")
    n_plane = lax.axis_size(PLANE)
    block, projected = pl.pallas_call(
        units_kernel,
        out_shape=(
            jax.ShapeDtypeStruct((BLOCK, width), jnp.bfloat16),
            jax.ShapeDtypeStruct((BLOCK, width), jnp.float32),
        ),
        in_specs=[SMEM] + [VMEM] * 5,
        out_specs=(VMEM, VMEM),
        scratch_shapes=[
            pltpu.VMEM((2 * BLOCK, depth), jnp.float32),
            pltpu.VMEM((BLOCK, width), jnp.float32),
        ],
        compiler_params=PARAMS,
        name="units",
    )(lengths, patch_keys, patch_values, probe_query.reshape(1, depth), projection, text_embeds)

    plane = lax.all_to_all(
        jnp.broadcast_to(block, (n_plane, BLOCK, width)), PLANE, 0, 0, tiled=True
    )
    line = lax.all_gather(block[None], "z", axis=0, tiled=True)
    parts = pl.pallas_call(
        lambda *refs: tile_kernel(count, *refs),
        out_shape=jax.ShapeDtypeStruct((n_plane * BLOCK, width), jnp.bfloat16),
        in_specs=[VMEM] * 3 + [SMEM] * 2,
        out_specs=VMEM,
        compiler_params=PARAMS,
        name="tile",
    )(
        plane.reshape(-1, width),
        line.reshape(-1, width),
        pair_group.reshape(-1, 128),
        logit_scale,
        logit_bias,
    )
    parts = lax.all_to_all(parts.reshape(n_plane, BLOCK, width), PLANE, 0, 0, tiled=True)
    return pl.pallas_call(
        grads_kernel,
        out_shape=(
            jax.ShapeDtypeStruct((count, depth), jnp.float32),
            jax.ShapeDtypeStruct((count, width), jnp.float32),
        ),
        in_specs=[VMEM] * 4,
        out_specs=(VMEM, VMEM),
        scratch_shapes=[pltpu.VMEM((BLOCK, width), jnp.float32)],
        compiler_params=PARAMS,
        name="grads",
    )(parts.reshape(-1, width), projected, projection, text_embeds)


def solution(mesh):
    fine = Mesh(mesh.devices.reshape(SIZES), AXES)
    rows = P(AXES, None)
    in_specs = (rows, rows, rows, P(), P(), rows, P(), P(), P())
    return jax.shard_map(
        shards, mesh=fine, in_specs=in_specs, out_specs=(rows, rows), check_vma=False
    )
```

```python
import math

import jax
import jax.numpy as jnp
from jax import lax
from jax.experimental import pallas as pl
from jax.experimental.pallas import tpu as pltpu
from jax.sharding import Mesh, PartitionSpec as P

H = 16
HD = 96

AXES = ("y_hi", "x", "core", "z_hi", "z_lo", "y_lo")
SIZES = (2, 4, 2, 8, 4, 2)
PLANE = ("y_hi", "x", "core", "y_lo")

BLOCK = 8
HALF = 4

epsilon = 1e-06
VMEM = pl.BlockSpec(memory_space=pltpu.VMEM)
SMEM = pl.BlockSpec(memory_space=pltpu.SMEM)
PARAMS = pltpu.CompilerParams(vmem_limit_bytes=24 << 20)


def row_norm(rows):
    return jnp.sqrt(jnp.sum(rows * rows, axis=1, keepdims=True) + epsilon)


def units_kernel(
    lengths, keys, values, probe, projection, text, block, projected, pooled, units
):
    n_rows, width = keys.shape
    head = lax.broadcasted_iota(jnp.int32, (H, width), 0)
    own = lax.broadcasted_iota(jnp.int32, (H, width), 1) // HD == head
    query = jnp.where(own, probe[...].astype(jnp.float32), 0.0).astype(jnp.bfloat16)
    scores = lax.dot_general(
        query, keys[...], (((1,), (1,)), ((), ())), preferred_element_type=jnp.float32
    ) / math.sqrt(HD)
    row = lax.broadcasted_iota(jnp.int32, (H, n_rows), 1)
    start = jnp.int32(0)
    weights = []
    for image in range(lengths.shape[1]):
        end = start + lengths[0, image]
        member = (row >= start) & (row < end)
        masked = jnp.where(member, scores, -jnp.inf)
        terms = jnp.exp(masked - jnp.max(masked, axis=1, keepdims=True))
        weights.append((terms / jnp.sum(terms, axis=1, keepdims=True)).astype(jnp.bfloat16))
        start = end
    mixed = jnp.dot(
        jnp.concatenate(weights), values[...], preferred_element_type=jnp.float32
    )
    pooled[...] = jnp.zeros_like(pooled)
    for image in range(lengths.shape[1]):
        part = mixed[image * H : (image + 1) * H]
        pooled[image : image + 1, :] = jnp.sum(jnp.where(own, part, 0.0), axis=0, keepdims=True)
    proj = jnp.dot(
        pooled[...].astype(jnp.bfloat16), projection[...], preferred_element_type=jnp.float32
    )[:BLOCK]
    projected[...] = proj
    units[...] = proj / row_norm(proj)
    text_wide = text[...].astype(jnp.float32)
    count = text.shape[0]
    units[HALF : HALF + count, :] = text_wide / row_norm(text_wide)
    filled = lax.broadcasted_iota(jnp.int32, units.shape, 0) % HALF < count
    block[...] = jnp.where(filled, units[...], 0.0).astype(jnp.bfloat16)


def pick(groups, positions, axis):
    n_rows, lanes = groups.shape
    n = positions.shape[axis]
    high, low = groups // 64, groups % 64
    pieces = []
    for digit in (high, low):
        digit = digit.astype(jnp.float32).astype(jnp.bfloat16)
        if axis == 0:
            lane = lax.broadcasted_iota(jnp.int32, (n, lanes), 1)
            hot = jnp.where(lane == positions % lanes, 1.0, 0.0).astype(jnp.bfloat16)
            found = lax.dot_general(
                hot, digit, (((1,), (1,)), ((), ())), preferred_element_type=jnp.float32
            )
            line = lax.broadcasted_iota(jnp.int32, (n, n_rows), 1)
        else:
            lane = lax.broadcasted_iota(jnp.int32, (lanes, n), 0)
            hot = jnp.where(lane == positions % lanes, 1.0, 0.0).astype(jnp.bfloat16)
            found = jnp.dot(digit, hot, preferred_element_type=jnp.float32)
            line = lax.broadcasted_iota(jnp.int32, (n_rows, n), 0)
        kept = jnp.where(line == positions // lanes, found, 0.0)
        pieces.append(jnp.sum(kept, axis=1 - axis, keepdims=True))
    return pieces[0] * 64.0 + pieces[1]


def tile_kernel(count, plane, line, groups, scale, bias, parts):
    n_x, n_core, n_far, n_near, n_y = (lax.axis_size(axis) for axis in AXES[1:])
    blk = (lax.axis_index("y_hi") * n_x + lax.axis_index("x")) * n_core + lax.axis_index("core")
    z = lax.axis_index("z_hi") * n_near + lax.axis_index("z_lo")
    per_blk = n_far * n_near * n_y * count
    at = lax.broadcasted_iota(jnp.int32, (plane.shape[0], 1), 0)
    member, slot = at // BLOCK, jnp.minimum(at % HALF, count - 1)
    plane_at = (
        member // n_y * per_blk
        + (z * n_y + member % n_y) * count
        + slot
    )
    plane_kind = at % BLOCK // HALF
    at = lax.broadcasted_iota(jnp.int32, (1, line.shape[0]), 1)
    member, slot = at // BLOCK, jnp.minimum(at % HALF, count - 1)
    member = member % n_far * n_near + member // n_far
    line_at = blk * per_blk + (member * n_y + lax.axis_index("y_lo")) * count + slot
    line_kind = at % BLOCK // HALF
    plane_ids = pick(groups[...], plane_at, 0)
    line_ids = pick(groups[...], line_at, 1)

    logits = (
        lax.dot_general(
            plane[...], line[...], (((1,), (1,)), ((), ())), preferred_element_type=jnp.float32
        )
        * scale[0]
        + bias[0]
    )
    labels = jnp.where(plane_ids == line_ids, 1.0, -1.0)
    coeffs = -labels * jax.nn.sigmoid(-labels * logits) * scale[0]
    coeffs = jnp.where(plane_kind != line_kind, coeffs, 0.0).astype(jnp.bfloat16)
    parts[...] = jnp.dot(coeffs, line[...], preferred_element_type=jnp.float32).astype(jnp.bfloat16)


def grads_kernel(parts, projected, projection, text, pooled_grad, text_grad, sums):
    count, width = text.shape
    total = parts[...].astype(jnp.float32).reshape(-1, BLOCK, width)
    total = jnp.sum(total, axis=0)
    sums[...] = total
    proj = projected[...]
    norm = row_norm(proj)
    u = proj / norm
    d_proj = (total - jnp.sum(total * u, axis=1, keepdims=True) * u) / norm
    d_proj = jnp.concatenate([d_proj, jnp.zeros_like(d_proj)]).astype(jnp.bfloat16)
    pooled_grad[...] = lax.dot_general(
        d_proj, projection[...], (((1,), (1,)), ((), ())), preferred_element_type=jnp.float32
    )[:count]
    text_wide = text[...].astype(jnp.float32)
    norm = row_norm(text_wide)
    v = text_wide / norm
    d_txt = sums[HALF : HALF + count, :]
    text_grad[...] = (d_txt - jnp.sum(d_txt * v, axis=1, keepdims=True) * v) / norm


def spread(rows, axis):
    n = lax.axis_size(axis)
    copies = jnp.broadcast_to(rows, (n,) + rows.shape)
    return lax.all_to_all(copies, axis, 0, 0, tiled=True).reshape(-1, rows.shape[1])


def shards(
    patch_keys,
    patch_values,
    lengths,
    probe_query,
    projection,
    text_embeds,
    pair_group,
    logit_scale,
    logit_bias,
):
    count, width = text_embeds.shape
    depth = patch_keys.shape[1]
    n_plane = lax.axis_size(PLANE)
    block, projected = pl.pallas_call(
        units_kernel,
        out_shape=(
            jax.ShapeDtypeStruct((BLOCK, width), jnp.bfloat16),
            jax.ShapeDtypeStruct((BLOCK, width), jnp.float32),
        ),
        in_specs=[SMEM] + [VMEM] * 5,
        out_specs=(VMEM, VMEM),
        scratch_shapes=[
            pltpu.VMEM((2 * BLOCK, depth), jnp.float32),
            pltpu.VMEM((BLOCK, width), jnp.float32),
        ],
        compiler_params=PARAMS,
        name="units",
    )(lengths, patch_keys, patch_values, probe_query.reshape(1, depth), projection, text_embeds)

    far = spread(block, "z_hi")
    plane = block
    for step, axis in enumerate(PLANE[::-1]):
        if step == 2:
            far, plane = lax.optimization_barrier((far, plane))
        plane = lax.all_gather(plane, axis, axis=0, tiled=True)
    line = spread(far, "z_lo")
    parts = pl.pallas_call(
        lambda *refs: tile_kernel(count, *refs),
        out_shape=jax.ShapeDtypeStruct((n_plane * BLOCK, width), jnp.bfloat16),
        in_specs=[VMEM] * 3 + [SMEM] * 2,
        out_specs=VMEM,
        compiler_params=PARAMS,
        name="tile",
    )(
        plane,
        line,
        pair_group.reshape(-1, 128),
        logit_scale,
        logit_bias,
    )
    parts = lax.all_to_all(parts.reshape(n_plane, BLOCK, width), PLANE, 0, 0, tiled=True)
    return pl.pallas_call(
        grads_kernel,
        out_shape=(
            jax.ShapeDtypeStruct((count, depth), jnp.float32),
            jax.ShapeDtypeStruct((count, width), jnp.float32),
        ),
        in_specs=[VMEM] * 4,
        out_specs=(VMEM, VMEM),
        scratch_shapes=[pltpu.VMEM((BLOCK, width), jnp.float32)],
        compiler_params=PARAMS,
        name="grads",
    )(parts.reshape(-1, width), projected, projection, text_embeds)


def solution(mesh):
    fine = Mesh(mesh.devices.reshape(SIZES), AXES)
    rows = P(AXES, None)
    in_specs = (rows, rows, rows, P(), P(), rows, P(), P(), P())
    return jax.shard_map(
        shards, mesh=fine, in_specs=in_specs, out_specs=(rows, rows), check_vma=False
    )
```

```python
import math

import jax
import jax.numpy as jnp
from jax import lax
from jax.experimental import pallas as pl
from jax.experimental.pallas import tpu as pltpu
from jax.sharding import Mesh, PartitionSpec as P

H = 16
HD = 96

AXES = ("y_hi", "x", "core", "z", "y_lo")
SIZES = (2, 4, 2, 32, 2)
PLANE = ("y_hi", "x", "core", "y_lo")

BLOCK = 8
HALF = 4
LANES = 128
SPARE = (3, 7)
FILLED = (0, 1, 2, 4, 5, 6)

epsilon = 1e-06
VMEM = pl.BlockSpec(memory_space=pltpu.VMEM)
SMEM = pl.BlockSpec(memory_space=pltpu.SMEM)
HBM = pl.BlockSpec(memory_space=pltpu.HBM)
PARAMS = pltpu.CompilerParams(vmem_limit_bytes=24 << 20)


def row_norm(rows):
    return jnp.sqrt(jnp.sum(rows * rows, axis=1, keepdims=True) + epsilon)


def pack(rows):
    main = rows.shape[2] - len(SPARE) * LANES
    place = lax.broadcasted_iota(jnp.int32, (rows.shape[0], BLOCK, LANES), 1)
    runs = []
    for run in range(main // LANES):
        here = rows[:, :, run * LANES : (run + 1) * LANES]
        for step, spare in enumerate(SPARE):
            if run < len(FILLED):
                at = main + step * LANES
                moved = rows[:, FILLED[run] : FILLED[run] + 1, at : at + LANES]
                here = jnp.where(place == spare, moved, here)
            else:
                here = jnp.where(place == spare, 0.0, here)
        runs.append(here)
    return jnp.concatenate(runs, axis=2)


def unpack(rows):
    place = lax.broadcasted_iota(jnp.int32, (rows.shape[0], BLOCK, LANES), 1)
    runs = []
    for run in range(rows.shape[2] // LANES):
        here = rows[:, :, run * LANES : (run + 1) * LANES]
        for spare in SPARE:
            here = jnp.where(place == spare, 0.0, here)
        runs.append(here)
    for spare in SPARE:
        tail = jnp.zeros(place.shape, rows.dtype)
        for run, filled in enumerate(FILLED):
            moved = rows[:, spare : spare + 1, run * LANES : (run + 1) * LANES]
            tail = jnp.where(place == filled, moved, tail)
        runs.append(tail)
    return jnp.concatenate(runs, axis=2)


def unpack_rows(rows):
    wide = unpack(rows.astype(jnp.float32).reshape(-1, BLOCK, rows.shape[1]))
    return wide.reshape(-1, wide.shape[2]).astype(jnp.bfloat16)


def units_kernel(
    lengths_at,
    keys_at,
    values_at,
    probe,
    projection_at,
    text_at,
    block,
    copies,
    projected,
    lengths,
    keys,
    values,
    projection,
    text,
    pooled,
    units,
    arrived,
):
    fetches = [
        pltpu.make_async_copy(source, target, arrived.at[i])
        for i, (source, target) in enumerate(
            (
                (lengths_at, lengths),
                (keys_at, keys),
                (values_at, values),
                (text_at, text),
                (projection_at, projection),
            )
        )
    ]
    for fetch in fetches:
        fetch.start()
    n_rows, width = keys.shape
    head = lax.broadcasted_iota(jnp.int32, (H, width), 0)
    own = lax.broadcasted_iota(jnp.int32, (H, width), 1) // HD == head
    query = jnp.where(own, probe[...].astype(jnp.float32), 0.0).astype(jnp.bfloat16)
    fetches[0].wait()
    fetches[1].wait()
    scores = lax.dot_general(
        query, keys[...], (((1,), (1,)), ((), ())), preferred_element_type=jnp.float32
    ) / math.sqrt(HD)
    row = lax.broadcasted_iota(jnp.int32, (H, n_rows), 1)
    start = jnp.int32(0)
    weights = []
    for image in range(lengths.shape[1]):
        end = start + lengths[0, image]
        member = (row >= start) & (row < end)
        masked = jnp.where(member, scores, -jnp.inf)
        terms = jnp.exp(masked - jnp.max(masked, axis=1, keepdims=True))
        weights.append((terms / jnp.sum(terms, axis=1, keepdims=True)).astype(jnp.bfloat16))
        start = end
    fetches[2].wait()
    mixed = jnp.dot(
        jnp.concatenate(weights), values[...], preferred_element_type=jnp.float32
    )
    pooled[...] = jnp.zeros_like(pooled)
    for image in range(lengths.shape[1]):
        part = mixed[image * H : (image + 1) * H]
        pooled[image : image + 1, :] = jnp.sum(jnp.where(own, part, 0.0), axis=0, keepdims=True)
    fetches[3].wait()
    fetches[4].wait()
    proj = jnp.dot(
        pooled[...].astype(jnp.bfloat16), projection[...], preferred_element_type=jnp.float32
    )[:BLOCK]
    projected[...] = proj
    units[...] = proj / row_norm(proj)
    text_wide = text[...].astype(jnp.float32)
    count = text.shape[0]
    units[HALF : HALF + count, :] = text_wide / row_norm(text_wide)
    packed = pack(units[...][None])
    block[...] = packed[0].astype(jnp.bfloat16)
    n = copies.shape[0] // BLOCK
    copies[...] = (
        jnp.broadcast_to(packed, (n,) + packed.shape[1:]).reshape(copies.shape).astype(jnp.bfloat16)
    )


def pick(groups, positions, axis):
    n_rows, lanes = groups.shape
    n = positions.shape[axis]
    high, low = groups // 64, groups % 64
    pieces = []
    for digit in (high, low):
        digit = digit.astype(jnp.float32).astype(jnp.bfloat16)
        if axis == 0:
            lane = lax.broadcasted_iota(jnp.int32, (n, lanes), 1)
            hot = jnp.where(lane == positions % lanes, 1.0, 0.0).astype(jnp.bfloat16)
            found = lax.dot_general(
                hot, digit, (((1,), (1,)), ((), ())), preferred_element_type=jnp.float32
            )
            line = lax.broadcasted_iota(jnp.int32, (n, n_rows), 1)
        else:
            lane = lax.broadcasted_iota(jnp.int32, (lanes, n), 0)
            hot = jnp.where(lane == positions % lanes, 1.0, 0.0).astype(jnp.bfloat16)
            found = jnp.dot(digit, hot, preferred_element_type=jnp.float32)
            line = lax.broadcasted_iota(jnp.int32, (n_rows, n), 0)
        kept = jnp.where(line == positions // lanes, found, 0.0)
        pieces.append(jnp.sum(kept, axis=1 - axis, keepdims=True))
    return pieces[0] * 64.0 + pieces[1]


def tile_kernel(count, plane, line, groups, scale, bias, parts):
    n_x, n_core, n_z, n_y = (lax.axis_size(axis) for axis in ("x", "core", "z", "y_lo"))
    blk = (lax.axis_index("y_hi") * n_x + lax.axis_index("x")) * n_core + lax.axis_index("core")
    per_blk = n_z * n_y * count
    at = lax.broadcasted_iota(jnp.int32, (plane.shape[0], 1), 0)
    member, slot = at // BLOCK, jnp.minimum(at % HALF, count - 1)
    plane_at = (
        member // n_y * per_blk
        + (lax.axis_index("z") * n_y + member % n_y) * count
        + slot
    )
    plane_kind = at % BLOCK // HALF
    at = lax.broadcasted_iota(jnp.int32, (1, line.shape[0]), 1)
    member, slot = at // BLOCK, jnp.minimum(at % HALF, count - 1)
    line_at = blk * per_blk + (member * n_y + lax.axis_index("y_lo")) * count + slot
    line_kind = at % BLOCK // HALF
    plane_ids = pick(groups[...], plane_at, 0)
    line_ids = pick(groups[...], line_at, 1)

    plane_rows, line_rows = unpack_rows(plane[...]), unpack_rows(line[...])
    logits = (
        lax.dot_general(
            plane_rows, line_rows, (((1,), (1,)), ((), ())), preferred_element_type=jnp.float32
        )
        * scale[0]
        + bias[0]
    )
    labels = jnp.where(plane_ids == line_ids, 1.0, -1.0)
    coeffs = -labels * jax.nn.sigmoid(-labels * logits) * scale[0]
    coeffs = jnp.where(plane_kind != line_kind, coeffs, 0.0).astype(jnp.bfloat16)
    wide = jnp.dot(coeffs, line_rows, preferred_element_type=jnp.float32)
    packed = pack(wide.reshape(-1, BLOCK, wide.shape[1]))
    parts[...] = packed.reshape(parts.shape).astype(jnp.bfloat16)


def grads_kernel(parts, projected, projection, text, pooled_grad, text_grad, sums):
    count, width = text.shape
    total = parts[...].astype(jnp.float32).reshape(-1, BLOCK, parts.shape[1])
    total = unpack(jnp.sum(total, axis=0, keepdims=True))[0]
    sums[...] = total
    proj = projected[...]
    norm = row_norm(proj)
    u = proj / norm
    d_proj = (total - jnp.sum(total * u, axis=1, keepdims=True) * u) / norm
    d_proj = jnp.concatenate([d_proj, jnp.zeros_like(d_proj)]).astype(jnp.bfloat16)
    pooled_grad[...] = lax.dot_general(
        d_proj, projection[...], (((1,), (1,)), ((), ())), preferred_element_type=jnp.float32
    )[:count]
    text_wide = text[...].astype(jnp.float32)
    norm = row_norm(text_wide)
    v = text_wide / norm
    d_txt = sums[HALF : HALF + count, :]
    text_grad[...] = (d_txt - jnp.sum(d_txt * v, axis=1, keepdims=True) * v) / norm


def shards(
    patch_keys,
    patch_values,
    lengths,
    probe_query,
    projection,
    text_embeds,
    pair_group,
    logit_scale,
    logit_bias,
):
    count, width = text_embeds.shape
    depth = patch_keys.shape[1]
    n_z = lax.axis_size("z")
    n_plane = lax.axis_size(PLANE)
    narrow = width - len(SPARE) * LANES
    block, copies, projected = pl.pallas_call(
        units_kernel,
        out_shape=(
            jax.ShapeDtypeStruct((BLOCK, narrow), jnp.bfloat16),
            jax.ShapeDtypeStruct((n_z * BLOCK, narrow), jnp.bfloat16),
            jax.ShapeDtypeStruct((BLOCK, width), jnp.float32),
        ),
        in_specs=[HBM] * 3 + [VMEM] + [HBM] * 2,
        out_specs=(VMEM, VMEM, VMEM),
        scratch_shapes=[
            pltpu.SMEM(lengths.shape, lengths.dtype),
            pltpu.VMEM(patch_keys.shape, patch_keys.dtype),
            pltpu.VMEM(patch_values.shape, patch_values.dtype),
            pltpu.VMEM(projection.shape, projection.dtype),
            pltpu.VMEM(text_embeds.shape, text_embeds.dtype),
            pltpu.VMEM((2 * BLOCK, depth), jnp.float32),
            pltpu.VMEM((BLOCK, width), jnp.float32),
            pltpu.SemaphoreType.DMA((5,)),
        ],
        compiler_params=pltpu.CompilerParams(vmem_limit_bytes=60 << 20),
        name="units",
    )(lengths, patch_keys, patch_values, probe_query.reshape(1, depth), projection, text_embeds)

    line = lax.all_to_all(copies.reshape(n_z, BLOCK, narrow), "z", 0, 0, tiled=True)
    plane = block
    for axis in PLANE[::-1]:
        plane = lax.all_gather(plane, axis, axis=0, tiled=True)
    parts = pl.pallas_call(
        lambda *refs: tile_kernel(count, *refs),
        out_shape=jax.ShapeDtypeStruct((n_plane * BLOCK, narrow), jnp.bfloat16),
        in_specs=[VMEM] * 3 + [SMEM] * 2,
        out_specs=VMEM,
        compiler_params=PARAMS,
        name="tile",
    )(
        plane,
        line.reshape(-1, narrow),
        pair_group.reshape(-1, 128),
        logit_scale,
        logit_bias,
    )
    parts = lax.all_to_all(parts.reshape(n_plane, BLOCK, narrow), PLANE, 0, 0, tiled=True)
    return pl.pallas_call(
        grads_kernel,
        out_shape=(
            jax.ShapeDtypeStruct((count, depth), jnp.float32),
            jax.ShapeDtypeStruct((count, width), jnp.float32),
        ),
        in_specs=[VMEM] * 4,
        out_specs=(VMEM, VMEM),
        scratch_shapes=[pltpu.VMEM((BLOCK, width), jnp.float32)],
        compiler_params=PARAMS,
        name="grads",
    )(parts.reshape(-1, narrow), projected, projection, text_embeds)


def solution(mesh):
    fine = Mesh(mesh.devices.reshape(SIZES), AXES)
    rows = P(AXES, None)
    in_specs = (rows, rows, rows, P(), P(), rows, P(), P(), P())
    return jax.shard_map(
        shards, mesh=fine, in_specs=in_specs, out_specs=(rows, rows), check_vma=False
    )
```

```python
import math

import jax
import jax.numpy as jnp
from jax import lax
from jax.experimental import pallas as pl
from jax.experimental.pallas import tpu as pltpu
from jax.sharding import Mesh, PartitionSpec as P

H = 16
HD = 96

AXES = ("y_hi", "x", "core", "z_hi", "z_lo", "y_lo")
SIZES = (2, 4, 2, 8, 4, 2)
PLANE = ("core", "y_hi", "y_lo", "x")

BLOCK = 8
HALF = 4
LANES = 128
SPARE = (3, 7)
FILLED = (0, 1, 2, 4, 5, 6)

epsilon = 1e-06
VMEM = pl.BlockSpec(memory_space=pltpu.VMEM)
SMEM = pl.BlockSpec(memory_space=pltpu.SMEM)
HBM = pl.BlockSpec(memory_space=pltpu.HBM)
PARAMS = pltpu.CompilerParams(vmem_limit_bytes=24 << 20)


def row_norm(rows):
    return jnp.sqrt(jnp.sum(rows * rows, axis=1, keepdims=True) + epsilon)


def pack(rows):
    main = rows.shape[2] - len(SPARE) * LANES
    place = lax.broadcasted_iota(jnp.int32, (rows.shape[0], BLOCK, LANES), 1)
    runs = []
    for run in range(main // LANES):
        here = rows[:, :, run * LANES : (run + 1) * LANES]
        for step, spare in enumerate(SPARE):
            if run < len(FILLED):
                at = main + step * LANES
                moved = rows[:, FILLED[run] : FILLED[run] + 1, at : at + LANES]
                here = jnp.where(place == spare, moved, here)
            else:
                here = jnp.where(place == spare, 0.0, here)
        runs.append(here)
    return jnp.concatenate(runs, axis=2)


def unpack(rows):
    place = lax.broadcasted_iota(jnp.int32, (rows.shape[0], BLOCK, LANES), 1)
    runs = []
    for run in range(rows.shape[2] // LANES):
        here = rows[:, :, run * LANES : (run + 1) * LANES]
        for spare in SPARE:
            here = jnp.where(place == spare, 0.0, here)
        runs.append(here)
    for spare in SPARE:
        tail = jnp.zeros(place.shape, rows.dtype)
        for run, filled in enumerate(FILLED):
            moved = rows[:, spare : spare + 1, run * LANES : (run + 1) * LANES]
            tail = jnp.where(place == filled, moved, tail)
        runs.append(tail)
    return jnp.concatenate(runs, axis=2)


def unpack_rows(rows):
    wide = unpack(rows.astype(jnp.float32).reshape(-1, BLOCK, rows.shape[1]))
    return wide.reshape(-1, wide.shape[2]).astype(jnp.bfloat16)


def units_kernel(
    lengths_at,
    keys_at,
    values_at,
    probe,
    projection_at,
    text_at,
    block,
    copies,
    projected,
    lengths,
    keys,
    values,
    projection,
    text,
    pooled,
    units,
    arrived,
):
    fetches = [
        pltpu.make_async_copy(source, target, arrived.at[i])
        for i, (source, target) in enumerate(
            (
                (lengths_at, lengths),
                (keys_at, keys),
                (values_at, values),
                (text_at, text),
                (projection_at, projection),
            )
        )
    ]
    for fetch in fetches:
        fetch.start()
    n_rows, width = keys.shape
    head = lax.broadcasted_iota(jnp.int32, (H, width), 0)
    own = lax.broadcasted_iota(jnp.int32, (H, width), 1) // HD == head
    query = jnp.where(own, probe[...].astype(jnp.float32).reshape(1, width), 0.0).astype(jnp.bfloat16)
    fetches[0].wait()
    fetches[1].wait()
    scores = lax.dot_general(
        query, keys[...], (((1,), (1,)), ((), ())), preferred_element_type=jnp.float32
    ) / math.sqrt(HD)
    row = lax.broadcasted_iota(jnp.int32, (H, n_rows), 1)
    start = jnp.int32(0)
    weights = []
    for image in range(lengths.shape[1]):
        end = start + lengths[0, image]
        member = (row >= start) & (row < end)
        masked = jnp.where(member, scores, -jnp.inf)
        terms = jnp.exp(masked - jnp.max(masked, axis=1, keepdims=True))
        weights.append((terms / jnp.sum(terms, axis=1, keepdims=True)).astype(jnp.bfloat16))
        start = end
    fetches[2].wait()
    mixed = jnp.dot(
        jnp.concatenate(weights), values[...], preferred_element_type=jnp.float32
    )
    pooled[...] = jnp.zeros_like(pooled)
    for image in range(lengths.shape[1]):
        part = mixed[image * H : (image + 1) * H]
        pooled[image : image + 1, :] = jnp.sum(jnp.where(own, part, 0.0), axis=0, keepdims=True)
    fetches[3].wait()
    fetches[4].wait()
    proj = jnp.dot(
        pooled[...].astype(jnp.bfloat16), projection[...], preferred_element_type=jnp.float32
    )[:BLOCK]
    projected[...] = proj
    units[...] = proj / row_norm(proj)
    text_wide = text[...].astype(jnp.float32)
    count = text.shape[0]
    units[HALF : HALF + count, :] = text_wide / row_norm(text_wide)
    packed = pack(units[...][None])
    block[...] = packed[0].astype(jnp.bfloat16)
    n = copies.shape[0] // BLOCK
    copies[...] = (
        jnp.broadcast_to(packed, (n,) + packed.shape[1:]).reshape(copies.shape).astype(jnp.bfloat16)
    )


def pick(groups, positions, axis):
    n_rows, lanes = groups.shape
    n = positions.shape[axis]
    high, low = groups // 64, groups % 64
    pieces = []
    for digit in (high, low):
        digit = digit.astype(jnp.float32).astype(jnp.bfloat16)
        if axis == 0:
            lane = lax.broadcasted_iota(jnp.int32, (n, lanes), 1)
            hot = jnp.where(lane == positions % lanes, 1.0, 0.0).astype(jnp.bfloat16)
            found = lax.dot_general(
                hot, digit, (((1,), (1,)), ((), ())), preferred_element_type=jnp.float32
            )
            line = lax.broadcasted_iota(jnp.int32, (n, n_rows), 1)
        else:
            lane = lax.broadcasted_iota(jnp.int32, (lanes, n), 0)
            hot = jnp.where(lane == positions % lanes, 1.0, 0.0).astype(jnp.bfloat16)
            found = jnp.dot(digit, hot, preferred_element_type=jnp.float32)
            line = lax.broadcasted_iota(jnp.int32, (n_rows, n), 0)
        kept = jnp.where(line == positions // lanes, found, 0.0)
        pieces.append(jnp.sum(kept, axis=1 - axis, keepdims=True))
    return pieces[0] * 64.0 + pieces[1]


def device(place, sizes):
    number = 0
    for axis in AXES:
        number = number * sizes[axis] + place[axis]
    return number


def tile_kernel(count, plane, line, groups, scale, bias, parts):
    sizes = dict((axis, lax.axis_size(axis)) for axis in AXES)
    place = dict((axis, lax.axis_index(axis)) for axis in AXES)
    at = lax.broadcasted_iota(jnp.int32, (plane.shape[0], 1), 0)
    member, slot = at // BLOCK, jnp.minimum(at % HALF, count - 1)
    there = dict(place)
    for axis in PLANE[::-1]:
        there[axis] = member % sizes[axis]
        member = member // sizes[axis]
    plane_at = device(there, sizes) * count + slot
    plane_kind = at % BLOCK // HALF
    at = lax.broadcasted_iota(jnp.int32, (1, line.shape[0]), 1)
    member, slot = at // BLOCK, jnp.minimum(at % HALF, count - 1)
    there = dict(place, z_hi=member % sizes["z_hi"], z_lo=member // sizes["z_hi"])
    line_at = device(there, sizes) * count + slot
    line_kind = at % BLOCK // HALF
    plane_ids = pick(groups[...], plane_at, 0)
    line_ids = pick(groups[...], line_at, 1)

    plane_rows, line_rows = unpack_rows(plane[...]), unpack_rows(line[...])
    logits = (
        lax.dot_general(
            plane_rows, line_rows, (((1,), (1,)), ((), ())), preferred_element_type=jnp.float32
        )
        * scale[0]
        + bias[0]
    )
    labels = jnp.where(plane_ids == line_ids, 1.0, -1.0)
    coeffs = -labels * jax.nn.sigmoid(-labels * logits) * scale[0]
    coeffs = jnp.where(plane_kind != line_kind, coeffs, 0.0).astype(jnp.bfloat16)
    wide = jnp.dot(coeffs, line_rows, preferred_element_type=jnp.float32)
    packed = pack(wide.reshape(-1, BLOCK, wide.shape[1]))
    parts[...] = packed.reshape(parts.shape).astype(jnp.bfloat16)


def grads_kernel(parts, projected, projection, text, pooled_grad, text_grad, sums):
    count, width = text.shape
    total = parts[...].astype(jnp.float32).reshape(-1, BLOCK, parts.shape[1])
    total = unpack(jnp.sum(total, axis=0, keepdims=True))[0]
    sums[...] = total
    proj = projected[...]
    norm = row_norm(proj)
    u = proj / norm
    d_proj = (total - jnp.sum(total * u, axis=1, keepdims=True) * u) / norm
    d_proj = jnp.concatenate([d_proj, jnp.zeros_like(d_proj)]).astype(jnp.bfloat16)
    pooled_grad[...] = lax.dot_general(
        d_proj, projection[...], (((1,), (1,)), ((), ())), preferred_element_type=jnp.float32
    )[:count]
    text_wide = text[...].astype(jnp.float32)
    norm = row_norm(text_wide)
    v = text_wide / norm
    d_txt = sums[HALF : HALF + count, :]
    text_grad[...] = (d_txt - jnp.sum(d_txt * v, axis=1, keepdims=True) * v) / norm


def exchange(rows, axis):
    shape = (lax.axis_size(axis), -1, rows.shape[1])
    return lax.all_to_all(rows.reshape(shape), axis, 0, 0, tiled=True).reshape(rows.shape)


def shards(
    patch_keys,
    patch_values,
    lengths,
    probe_query,
    projection,
    text_embeds,
    pair_group,
    logit_scale,
    logit_bias,
):
    count, width = text_embeds.shape
    depth = patch_keys.shape[1]
    n_far = lax.axis_size("z_hi")
    n_plane = lax.axis_size(PLANE)
    narrow = width - len(SPARE) * LANES
    block, copies, projected = pl.pallas_call(
        units_kernel,
        out_shape=(
            jax.ShapeDtypeStruct((BLOCK, narrow), jnp.bfloat16),
            jax.ShapeDtypeStruct((n_far * BLOCK, narrow), jnp.bfloat16),
            jax.ShapeDtypeStruct((BLOCK, width), jnp.float32),
        ),
        in_specs=[HBM] * 3 + [VMEM] + [HBM] * 2,
        out_specs=(VMEM, VMEM, VMEM),
        scratch_shapes=[
            pltpu.SMEM(lengths.shape, lengths.dtype),
            pltpu.VMEM(patch_keys.shape, patch_keys.dtype),
            pltpu.VMEM(patch_values.shape, patch_values.dtype),
            pltpu.VMEM(projection.shape, projection.dtype),
            pltpu.VMEM(text_embeds.shape, text_embeds.dtype),
            pltpu.VMEM((2 * BLOCK, depth), jnp.float32),
            pltpu.VMEM((BLOCK, width), jnp.float32),
            pltpu.SemaphoreType.DMA((5,)),
        ],
        compiler_params=pltpu.CompilerParams(vmem_limit_bytes=60 << 20),
        name="units",
    )(lengths, patch_keys, patch_values, probe_query, projection, text_embeds)

    far = exchange(copies, "z_hi")
    plane = block
    for step, axis in enumerate(PLANE[::-1]):
        if step == 2:
            far, plane = lax.optimization_barrier((far, plane))
        plane = lax.all_gather(plane, axis, axis=0, tiled=True)
    line = exchange(jnp.tile(far, (lax.axis_size("z_lo"), 1)), "z_lo")
    parts = pl.pallas_call(
        lambda *refs: tile_kernel(count, *refs),
        out_shape=jax.ShapeDtypeStruct((n_plane * BLOCK, narrow), jnp.bfloat16),
        in_specs=[VMEM] * 3 + [SMEM] * 2,
        out_specs=VMEM,
        compiler_params=pltpu.CompilerParams(vmem_limit_bytes=60 << 20),
        name="tile",
    )(
        plane,
        line,
        pair_group.reshape(-1, 128),
        logit_scale,
        logit_bias,
    )
    parts = exchange(parts, PLANE)
    return pl.pallas_call(
        grads_kernel,
        out_shape=(
            jax.ShapeDtypeStruct((count, depth), jnp.float32),
            jax.ShapeDtypeStruct((count, width), jnp.float32),
        ),
        in_specs=[VMEM] * 4,
        out_specs=(VMEM, VMEM),
        scratch_shapes=[pltpu.VMEM((BLOCK, width), jnp.float32)],
        compiler_params=PARAMS,
        name="grads",
    )(parts, projected, projection, text_embeds)


def solution(mesh):
    fine = Mesh(mesh.devices.reshape(SIZES), AXES)
    rows = P(AXES, None)
    in_specs = (rows, rows, rows, P(), P(), rows, P(), P(), P())
    return jax.shard_map(
        shards, mesh=fine, in_specs=in_specs, out_specs=(rows, rows), check_vma=False
    )
```

```python
import math

import jax
import jax.numpy as jnp
from jax import lax
from jax.experimental import pallas as pl
from jax.experimental.pallas import tpu as pltpu
from jax.sharding import Mesh, PartitionSpec as P

H = 16
HD = 96

AXES = ("y_hi", "x_hi", "x_lo", "core", "z_hi", "z_lo", "y_lo")
SIZES = (2, 2, 2, 2, 8, 4, 2)
PLANE = ("core", "y_hi", "x_hi", "y_lo", "x_lo")

BLOCK = 8
HALF = 4
LANES = 128
SPARE = (3, 7)
FILLED = (0, 1, 2, 4, 5, 6)
PARTS = 4

epsilon = 1e-06
VMEM = pl.BlockSpec(memory_space=pltpu.VMEM)
SMEM = pl.BlockSpec(memory_space=pltpu.SMEM)
HBM = pl.BlockSpec(memory_space=pltpu.HBM)
PARAMS = pltpu.CompilerParams(vmem_limit_bytes=24 << 20)


def row_norm(rows):
    return jnp.sqrt(jnp.sum(rows * rows, axis=1, keepdims=True) + epsilon)


def pack(rows):
    main = rows.shape[2] - len(SPARE) * LANES
    place = lax.broadcasted_iota(jnp.int32, (rows.shape[0], BLOCK, LANES), 1)
    runs = []
    for run in range(main // LANES):
        here = rows[:, :, run * LANES : (run + 1) * LANES]
        for step, spare in enumerate(SPARE):
            if run < len(FILLED):
                at = main + step * LANES
                moved = rows[:, FILLED[run] : FILLED[run] + 1, at : at + LANES]
                here = jnp.where(place == spare, moved, here)
            else:
                here = jnp.where(place == spare, 0.0, here)
        runs.append(here)
    return jnp.concatenate(runs, axis=2)


def unpack(rows):
    place = lax.broadcasted_iota(jnp.int32, (rows.shape[0], BLOCK, LANES), 1)
    runs = []
    for run in range(rows.shape[2] // LANES):
        here = rows[:, :, run * LANES : (run + 1) * LANES]
        for spare in SPARE:
            here = jnp.where(place == spare, 0.0, here)
        runs.append(here)
    for spare in SPARE:
        tail = jnp.zeros(place.shape, rows.dtype)
        for run, filled in enumerate(FILLED):
            moved = rows[:, spare : spare + 1, run * LANES : (run + 1) * LANES]
            tail = jnp.where(place == filled, moved, tail)
        runs.append(tail)
    return jnp.concatenate(runs, axis=2)


def unpack_rows(rows):
    wide = unpack(rows.astype(jnp.float32).reshape(-1, BLOCK, rows.shape[1]))
    return wide.reshape(-1, wide.shape[2]).astype(jnp.bfloat16)


def units_kernel(
    lengths_at,
    keys_at,
    values_at,
    probe,
    projection_at,
    text_at,
    block,
    copies,
    projected,
    lengths,
    keys,
    values,
    projection,
    text,
    pooled,
    units,
    arrived,
):
    deep = projection.shape[0] // PARTS
    fetches = [
        pltpu.make_async_copy(source, target, arrived.at[i])
        for i, (source, target) in enumerate(
            [
                (lengths_at, lengths),
                (keys_at, keys),
                (values_at, values),
                (text_at, text),
            ]
            + [
                (projection_at.at[pl.ds(part * deep, deep)], projection.at[pl.ds(part * deep, deep)])
                for part in range(PARTS)
            ]
        )
    ]
    for fetch in fetches:
        fetch.start()
    n_rows, width = keys.shape
    head = lax.broadcasted_iota(jnp.int32, (H, width), 0)
    own = lax.broadcasted_iota(jnp.int32, (H, width), 1) // HD == head
    query = jnp.where(own, probe[...].astype(jnp.float32).reshape(1, width), 0.0).astype(jnp.bfloat16)
    fetches[0].wait()
    fetches[1].wait()
    scores = lax.dot_general(
        query, keys[...], (((1,), (1,)), ((), ())), preferred_element_type=jnp.float32
    ) / math.sqrt(HD)
    row = lax.broadcasted_iota(jnp.int32, (H, n_rows), 1)
    start = jnp.int32(0)
    weights = []
    for image in range(lengths.shape[1]):
        end = start + lengths[0, image]
        member = (row >= start) & (row < end)
        masked = jnp.where(member, scores, -jnp.inf)
        terms = jnp.exp(masked - jnp.max(masked, axis=1, keepdims=True))
        weights.append((terms / jnp.sum(terms, axis=1, keepdims=True)).astype(jnp.bfloat16))
        start = end
    fetches[2].wait()
    mixed = jnp.dot(
        jnp.concatenate(weights), values[...], preferred_element_type=jnp.float32
    )
    pooled[...] = jnp.zeros_like(pooled)
    for image in range(lengths.shape[1]):
        part = mixed[image * H : (image + 1) * H]
        pooled[image : image + 1, :] = jnp.sum(jnp.where(own, part, 0.0), axis=0, keepdims=True)
    proj = jnp.zeros((2 * BLOCK, projected.shape[1]), jnp.float32)
    for part in range(PARTS):
        fetches[4 + part].wait()
        here = slice(part * deep, (part + 1) * deep)
        proj += jnp.dot(
            pooled[:, here].astype(jnp.bfloat16),
            projection[here, :],
            preferred_element_type=jnp.float32,
        )
    proj = proj[:BLOCK]
    fetches[3].wait()
    projected[...] = proj
    units[...] = proj / row_norm(proj)
    text_wide = text[...].astype(jnp.float32)
    count = text.shape[0]
    units[HALF : HALF + count, :] = text_wide / row_norm(text_wide)
    packed = pack(units[...][None])
    block[...] = packed[0].astype(jnp.bfloat16)
    n = copies.shape[0] // BLOCK
    copies[...] = (
        jnp.broadcast_to(packed, (n,) + packed.shape[1:]).reshape(copies.shape).astype(jnp.bfloat16)
    )


def pick(groups, positions, axis):
    n_rows, lanes = groups.shape
    n = positions.shape[axis]
    high, low = groups // 64, groups % 64
    pieces = []
    for digit in (high, low):
        digit = digit.astype(jnp.float32).astype(jnp.bfloat16)
        if axis == 0:
            lane = lax.broadcasted_iota(jnp.int32, (n, lanes), 1)
            hot = jnp.where(lane == positions % lanes, 1.0, 0.0).astype(jnp.bfloat16)
            found = lax.dot_general(
                hot, digit, (((1,), (1,)), ((), ())), preferred_element_type=jnp.float32
            )
            line = lax.broadcasted_iota(jnp.int32, (n, n_rows), 1)
        else:
            lane = lax.broadcasted_iota(jnp.int32, (lanes, n), 0)
            hot = jnp.where(lane == positions % lanes, 1.0, 0.0).astype(jnp.bfloat16)
            found = jnp.dot(digit, hot, preferred_element_type=jnp.float32)
            line = lax.broadcasted_iota(jnp.int32, (n_rows, n), 0)
        kept = jnp.where(line == positions // lanes, found, 0.0)
        pieces.append(jnp.sum(kept, axis=1 - axis, keepdims=True))
    return pieces[0] * 64.0 + pieces[1]


def device(place, sizes):
    number = 0
    for axis in AXES:
        number = number * sizes[axis] + place[axis]
    return number


def tile_kernel(count, plane, line, groups, scale, bias, parts):
    sizes = dict((axis, lax.axis_size(axis)) for axis in AXES)
    place = dict((axis, lax.axis_index(axis)) for axis in AXES)
    at = lax.broadcasted_iota(jnp.int32, (plane.shape[0], 1), 0)
    member, slot = at // BLOCK, jnp.minimum(at % HALF, count - 1)
    there = dict(place)
    for axis in PLANE[::-1]:
        there[axis] = member % sizes[axis]
        member = member // sizes[axis]
    plane_at = device(there, sizes) * count + slot
    plane_kind = at % BLOCK // HALF
    at = lax.broadcasted_iota(jnp.int32, (1, line.shape[0]), 1)
    member, slot = at // BLOCK, jnp.minimum(at % HALF, count - 1)
    there = dict(place, z_hi=member % sizes["z_hi"], z_lo=member // sizes["z_hi"])
    line_at = device(there, sizes) * count + slot
    line_kind = at % BLOCK // HALF
    plane_ids = pick(groups[...], plane_at, 0)
    line_ids = pick(groups[...], line_at, 1)

    plane_rows, line_rows = unpack_rows(plane[...]), unpack_rows(line[...])
    logits = (
        lax.dot_general(
            plane_rows, line_rows, (((1,), (1,)), ((), ())), preferred_element_type=jnp.float32
        )
        * scale[0]
        + bias[0]
    )
    labels = jnp.where(plane_ids == line_ids, 1.0, -1.0)
    coeffs = -labels * jax.nn.sigmoid(-labels * logits) * scale[0]
    coeffs = jnp.where(plane_kind != line_kind, coeffs, 0.0).astype(jnp.bfloat16)
    wide = jnp.dot(coeffs, line_rows, preferred_element_type=jnp.float32)
    packed = pack(wide.reshape(-1, BLOCK, wide.shape[1]))
    parts[...] = packed.reshape(parts.shape).astype(jnp.bfloat16)


def grads_kernel(parts, projected, projection, text, pooled_grad, text_grad, sums):
    count, width = text.shape
    total = parts[...].astype(jnp.float32).reshape(-1, BLOCK, parts.shape[1])
    total = unpack(jnp.sum(total, axis=0, keepdims=True))[0]
    sums[...] = total
    proj = projected[...]
    norm = row_norm(proj)
    u = proj / norm
    d_proj = (total - jnp.sum(total * u, axis=1, keepdims=True) * u) / norm
    d_proj = jnp.concatenate([d_proj, jnp.zeros_like(d_proj)]).astype(jnp.bfloat16)
    pooled_grad[...] = lax.dot_general(
        d_proj, projection[...], (((1,), (1,)), ((), ())), preferred_element_type=jnp.float32
    )[:count]
    text_wide = text[...].astype(jnp.float32)
    norm = row_norm(text_wide)
    v = text_wide / norm
    d_txt = sums[HALF : HALF + count, :]
    text_grad[...] = (d_txt - jnp.sum(d_txt * v, axis=1, keepdims=True) * v) / norm


def exchange(rows, axis):
    shape = (lax.axis_size(axis), -1, rows.shape[1])
    return lax.all_to_all(rows.reshape(shape), axis, 0, 0, tiled=True).reshape(rows.shape)


def shards(
    patch_keys,
    patch_values,
    lengths,
    probe_query,
    projection,
    text_embeds,
    pair_group,
    logit_scale,
    logit_bias,
):
    count, width = text_embeds.shape
    depth = patch_keys.shape[1]
    n_far = lax.axis_size("z_hi")
    n_plane = lax.axis_size(PLANE)
    narrow = width - len(SPARE) * LANES
    block, copies, projected = pl.pallas_call(
        units_kernel,
        out_shape=(
            jax.ShapeDtypeStruct((BLOCK, narrow), jnp.bfloat16),
            jax.ShapeDtypeStruct((n_far * BLOCK, narrow), jnp.bfloat16),
            jax.ShapeDtypeStruct((BLOCK, width), jnp.float32),
        ),
        in_specs=[HBM] * 3 + [VMEM] + [HBM] * 2,
        out_specs=(VMEM, VMEM, VMEM),
        scratch_shapes=[
            pltpu.SMEM(lengths.shape, lengths.dtype),
            pltpu.VMEM(patch_keys.shape, patch_keys.dtype),
            pltpu.VMEM(patch_values.shape, patch_values.dtype),
            pltpu.VMEM(projection.shape, projection.dtype),
            pltpu.VMEM(text_embeds.shape, text_embeds.dtype),
            pltpu.VMEM((2 * BLOCK, depth), jnp.float32),
            pltpu.VMEM((BLOCK, width), jnp.float32),
            pltpu.SemaphoreType.DMA((4 + PARTS,)),
        ],
        compiler_params=pltpu.CompilerParams(vmem_limit_bytes=60 << 20),
        name="units",
    )(lengths, patch_keys, patch_values, probe_query, projection, text_embeds)

    far = exchange(copies, "z_hi")
    plane = block
    for step, axis in enumerate(PLANE[::-1]):
        if step == 3:
            far, plane = lax.optimization_barrier((far, plane))
        plane = lax.all_gather(plane, axis, axis=0, tiled=True)
    line = exchange(jnp.tile(far, (lax.axis_size("z_lo"), 1)), "z_lo")
    parts = pl.pallas_call(
        lambda *refs: tile_kernel(count, *refs),
        out_shape=jax.ShapeDtypeStruct((n_plane * BLOCK, narrow), jnp.bfloat16),
        in_specs=[VMEM] * 3 + [SMEM] * 2,
        out_specs=VMEM,
        compiler_params=pltpu.CompilerParams(vmem_limit_bytes=60 << 20),
        name="tile",
    )(
        plane,
        line,
        pair_group.reshape(-1, 128),
        logit_scale,
        logit_bias,
    )
    parts = exchange(parts, PLANE)
    return pl.pallas_call(
        grads_kernel,
        out_shape=(
            jax.ShapeDtypeStruct((count, depth), jnp.float32),
            jax.ShapeDtypeStruct((count, width), jnp.float32),
        ),
        in_specs=[VMEM] * 4,
        out_specs=(VMEM, VMEM),
        scratch_shapes=[pltpu.VMEM((BLOCK, width), jnp.float32)],
        compiler_params=PARAMS,
        name="grads",
    )(parts, projected, projection, text_embeds)


def solution(mesh):
    fine = Mesh(mesh.devices.reshape(SIZES), AXES)
    rows = P(AXES, None)
    in_specs = (rows, rows, rows, P(), P(), rows, P(), P(), P())
    return jax.shard_map(
        shards, mesh=fine, in_specs=in_specs, out_specs=(rows, rows), check_vma=False
    )
```

```python
import math

import jax
import jax.numpy as jnp
from jax import lax
from jax.experimental import pallas as pl
from jax.experimental.pallas import tpu as pltpu
from jax.sharding import Mesh, PartitionSpec as P

H = 16
HD = 96

AXES = ("y_hi", "x_hi", "x_lo", "core", "z_hi", "z_lo", "y_lo")
SIZES = (2, 2, 2, 2, 8, 4, 2)
PLANE = ("core", "y_hi", "x_hi", "y_lo", "x_lo")

BLOCK = 8
HALF = 4
LANES = 128
SPARE = (3, 7)
FILLED = (0, 1, 2, 4, 5, 6)
PARTS = 4

epsilon = 1e-06
VMEM = pl.BlockSpec(memory_space=pltpu.VMEM)
SMEM = pl.BlockSpec(memory_space=pltpu.SMEM)
HBM = pl.BlockSpec(memory_space=pltpu.HBM)
PARAMS = pltpu.CompilerParams(vmem_limit_bytes=24 << 20)


def row_norm(rows):
    return jnp.sqrt(jnp.sum(rows * rows, axis=1, keepdims=True) + epsilon)


def pack(rows):
    main = rows.shape[2] - len(SPARE) * LANES
    place = lax.broadcasted_iota(jnp.int32, (rows.shape[0], BLOCK, LANES), 1)
    runs = []
    for run in range(main // LANES):
        here = rows[:, :, run * LANES : (run + 1) * LANES]
        for step, spare in enumerate(SPARE):
            if run < len(FILLED):
                at = main + step * LANES
                moved = rows[:, FILLED[run] : FILLED[run] + 1, at : at + LANES]
                here = jnp.where(place == spare, moved, here)
            else:
                here = jnp.where(place == spare, 0.0, here)
        runs.append(here)
    return jnp.concatenate(runs, axis=2)


def unpack(rows):
    place = lax.broadcasted_iota(jnp.int32, (rows.shape[0], BLOCK, LANES), 1)
    runs = []
    for run in range(rows.shape[2] // LANES):
        here = rows[:, :, run * LANES : (run + 1) * LANES]
        for spare in SPARE:
            here = jnp.where(place == spare, 0.0, here)
        runs.append(here)
    for spare in SPARE:
        tail = jnp.zeros(place.shape, rows.dtype)
        for run, filled in enumerate(FILLED):
            moved = rows[:, spare : spare + 1, run * LANES : (run + 1) * LANES]
            tail = jnp.where(place == filled, moved, tail)
        runs.append(tail)
    return jnp.concatenate(runs, axis=2)


def unpack_rows(rows):
    wide = unpack(rows.astype(jnp.float32).reshape(-1, BLOCK, rows.shape[1]))
    return wide.reshape(-1, wide.shape[2]).astype(jnp.bfloat16)


def units_kernel(
    lengths_at,
    keys_at,
    values_at,
    probe,
    projection_at,
    text_at,
    block,
    copies,
    projected,
    lengths,
    keys,
    values,
    projection,
    text,
    pooled,
    units,
    arrived,
):
    deep = projection.shape[0] // PARTS
    fetches = [
        pltpu.make_async_copy(source, target, arrived.at[i])
        for i, (source, target) in enumerate(
            [
                (lengths_at, lengths),
                (keys_at, keys),
                (values_at, values),
                (text_at, text),
            ]
            + [
                (projection_at.at[pl.ds(part * deep, deep)], projection.at[pl.ds(part * deep, deep)])
                for part in range(PARTS)
            ]
        )
    ]
    for fetch in fetches:
        fetch.start()
    n_rows, width = keys.shape
    head = lax.broadcasted_iota(jnp.int32, (H, width), 0)
    own = lax.broadcasted_iota(jnp.int32, (H, width), 1) // HD == head
    query = jnp.where(own, probe[...].astype(jnp.float32).reshape(1, width), 0.0).astype(jnp.bfloat16)
    fetches[0].wait()
    fetches[1].wait()
    scores = lax.dot_general(
        query, keys[...], (((1,), (1,)), ((), ())), preferred_element_type=jnp.float32
    ) / math.sqrt(HD)
    row = lax.broadcasted_iota(jnp.int32, (H, n_rows), 1)
    start = jnp.int32(0)
    weights = []
    for image in range(lengths.shape[1]):
        end = start + lengths[0, image]
        member = (row >= start) & (row < end)
        masked = jnp.where(member, scores, -jnp.inf)
        terms = jnp.exp(masked - jnp.max(masked, axis=1, keepdims=True))
        weights.append((terms / jnp.sum(terms, axis=1, keepdims=True)).astype(jnp.bfloat16))
        start = end
    fetches[2].wait()
    mixed = jnp.dot(
        jnp.concatenate(weights), values[...], preferred_element_type=jnp.float32
    )
    pooled[...] = jnp.zeros_like(pooled)
    for image in range(lengths.shape[1]):
        part = mixed[image * H : (image + 1) * H]
        pooled[image : image + 1, :] = jnp.sum(jnp.where(own, part, 0.0), axis=0, keepdims=True)
    proj = jnp.zeros((2 * BLOCK, projected.shape[1]), jnp.float32)
    for part in range(PARTS):
        fetches[4 + part].wait()
        here = slice(part * deep, (part + 1) * deep)
        proj += jnp.dot(
            pooled[:, here].astype(jnp.bfloat16),
            projection[here, :],
            preferred_element_type=jnp.float32,
        )
    proj = proj[:BLOCK]
    fetches[3].wait()
    projected[...] = proj
    units[...] = proj / row_norm(proj)
    text_wide = text[...].astype(jnp.float32)
    count = text.shape[0]
    units[HALF : HALF + count, :] = text_wide / row_norm(text_wide)
    packed = pack(units[...][None])
    block[...] = packed[0].astype(jnp.bfloat16)
    n = copies.shape[0] // BLOCK
    copies[...] = (
        jnp.broadcast_to(packed, (n,) + packed.shape[1:]).reshape(copies.shape).astype(jnp.bfloat16)
    )


def pick(groups, positions, axis):
    n_rows, lanes = groups.shape
    n = positions.shape[axis]
    high, low = groups // 64, groups % 64
    pieces = []
    for digit in (high, low):
        digit = digit.astype(jnp.float32).astype(jnp.bfloat16)
        if axis == 0:
            lane = lax.broadcasted_iota(jnp.int32, (n, lanes), 1)
            hot = jnp.where(lane == positions % lanes, 1.0, 0.0).astype(jnp.bfloat16)
            found = lax.dot_general(
                hot, digit, (((1,), (1,)), ((), ())), preferred_element_type=jnp.float32
            )
            line = lax.broadcasted_iota(jnp.int32, (n, n_rows), 1)
        else:
            lane = lax.broadcasted_iota(jnp.int32, (lanes, n), 0)
            hot = jnp.where(lane == positions % lanes, 1.0, 0.0).astype(jnp.bfloat16)
            found = jnp.dot(digit, hot, preferred_element_type=jnp.float32)
            line = lax.broadcasted_iota(jnp.int32, (n_rows, n), 0)
        kept = jnp.where(line == positions // lanes, found, 0.0)
        pieces.append(jnp.sum(kept, axis=1 - axis, keepdims=True))
    return pieces[0] * 64.0 + pieces[1]


def device(place, sizes):
    number = 0
    for axis in AXES:
        number = number * sizes[axis] + place[axis]
    return number


def tile_kernel(count, plane, *refs):
    *lines, groups, scale, bias, parts = refs
    line = jnp.concatenate([unpack_rows(rows[...]) for rows in lines])
    sizes = dict((axis, lax.axis_size(axis)) for axis in AXES)
    place = dict((axis, lax.axis_index(axis)) for axis in AXES)
    at = lax.broadcasted_iota(jnp.int32, (plane.shape[0], 1), 0)
    member, slot = at // BLOCK, jnp.minimum(at % HALF, count - 1)
    there = dict(place)
    for axis in PLANE[::-1]:
        there[axis] = member % sizes[axis]
        member = member // sizes[axis]
    plane_at = device(there, sizes) * count + slot
    plane_kind = at % BLOCK // HALF
    at = lax.broadcasted_iota(jnp.int32, (1, line.shape[0]), 1)
    member, slot = at // BLOCK, jnp.minimum(at % HALF, count - 1)
    behind = place["z_lo"] - member // sizes["z_hi"] + sizes["z_lo"]
    there = dict(place, z_hi=member % sizes["z_hi"], z_lo=behind % sizes["z_lo"])
    line_at = device(there, sizes) * count + slot
    line_kind = at % BLOCK // HALF
    plane_ids = pick(groups[...], plane_at, 0)
    line_ids = pick(groups[...], line_at, 1)

    plane_rows = unpack_rows(plane[...])
    logits = (
        lax.dot_general(
            plane_rows, line, (((1,), (1,)), ((), ())), preferred_element_type=jnp.float32
        )
        * scale[0]
        + bias[0]
    )
    labels = jnp.where(plane_ids == line_ids, 1.0, -1.0)
    coeffs = -labels * jax.nn.sigmoid(-labels * logits) * scale[0]
    coeffs = jnp.where(plane_kind != line_kind, coeffs, 0.0).astype(jnp.bfloat16)
    wide = jnp.dot(coeffs, line, preferred_element_type=jnp.float32)
    packed = pack(wide.reshape(-1, BLOCK, wide.shape[1]))
    parts[...] = packed.reshape(parts.shape).astype(jnp.bfloat16)


def grads_kernel(parts, projected, projection, text, pooled_grad, text_grad, sums):
    count, width = text.shape
    total = parts[...].astype(jnp.float32).reshape(-1, BLOCK, parts.shape[1])
    total = unpack(jnp.sum(total, axis=0, keepdims=True))[0]
    sums[...] = total
    proj = projected[...]
    norm = row_norm(proj)
    u = proj / norm
    d_proj = (total - jnp.sum(total * u, axis=1, keepdims=True) * u) / norm
    d_proj = jnp.concatenate([d_proj, jnp.zeros_like(d_proj)]).astype(jnp.bfloat16)
    pooled_grad[...] = lax.dot_general(
        d_proj, projection[...], (((1,), (1,)), ((), ())), preferred_element_type=jnp.float32
    )[:count]
    text_wide = text[...].astype(jnp.float32)
    norm = row_norm(text_wide)
    v = text_wide / norm
    d_txt = sums[HALF : HALF + count, :]
    text_grad[...] = (d_txt - jnp.sum(d_txt * v, axis=1, keepdims=True) * v) / norm


def exchange(rows, axis):
    shape = (lax.axis_size(axis), -1, rows.shape[1])
    return lax.all_to_all(rows.reshape(shape), axis, 0, 0, tiled=True).reshape(rows.shape)


def shards(
    patch_keys,
    patch_values,
    lengths,
    probe_query,
    projection,
    text_embeds,
    pair_group,
    logit_scale,
    logit_bias,
):
    count, width = text_embeds.shape
    depth = patch_keys.shape[1]
    n_far = lax.axis_size("z_hi")
    n_plane = lax.axis_size(PLANE)
    narrow = width - len(SPARE) * LANES
    block, copies, projected = pl.pallas_call(
        units_kernel,
        out_shape=(
            jax.ShapeDtypeStruct((BLOCK, narrow), jnp.bfloat16),
            jax.ShapeDtypeStruct((n_far * BLOCK, narrow), jnp.bfloat16),
            jax.ShapeDtypeStruct((BLOCK, width), jnp.float32),
        ),
        in_specs=[HBM] * 3 + [VMEM] + [HBM] * 2,
        out_specs=(VMEM, VMEM, VMEM),
        scratch_shapes=[
            pltpu.SMEM(lengths.shape, lengths.dtype),
            pltpu.VMEM(patch_keys.shape, patch_keys.dtype),
            pltpu.VMEM(patch_values.shape, patch_values.dtype),
            pltpu.VMEM(projection.shape, projection.dtype),
            pltpu.VMEM(text_embeds.shape, text_embeds.dtype),
            pltpu.VMEM((2 * BLOCK, depth), jnp.float32),
            pltpu.VMEM((BLOCK, width), jnp.float32),
            pltpu.SemaphoreType.DMA((4 + PARTS,)),
        ],
        compiler_params=pltpu.CompilerParams(vmem_limit_bytes=60 << 20),
        name="units",
    )(lengths, patch_keys, patch_values, probe_query, projection, text_embeds)

    far = exchange(copies, "z_hi")
    plane = block
    for axis in PLANE[::-1]:
        plane = lax.all_gather(plane, axis, axis=0, tiled=True)
    far, plane = lax.optimization_barrier((far, plane))
    n_near = lax.axis_size("z_lo")
    lines = [far]
    for ahead in range(1, n_near):
        route = [(i, (i + ahead) % n_near) for i in range(n_near)]
        lines.append(lax.ppermute(far, "z_lo", route))
    parts = pl.pallas_call(
        lambda *refs: tile_kernel(count, *refs),
        out_shape=jax.ShapeDtypeStruct((n_plane * BLOCK, narrow), jnp.bfloat16),
        in_specs=[VMEM] * (2 + n_near) + [SMEM] * 2,
        out_specs=VMEM,
        compiler_params=PARAMS,
        name="tile",
    )(
        plane,
        *lines,
        pair_group.reshape(-1, 128),
        logit_scale,
        logit_bias,
    )
    parts = exchange(parts, PLANE)
    return pl.pallas_call(
        grads_kernel,
        out_shape=(
            jax.ShapeDtypeStruct((count, depth), jnp.float32),
            jax.ShapeDtypeStruct((count, width), jnp.float32),
        ),
        in_specs=[VMEM] * 4,
        out_specs=(VMEM, VMEM),
        scratch_shapes=[pltpu.VMEM((BLOCK, width), jnp.float32)],
        compiler_params=PARAMS,
        name="grads",
    )(parts, projected, projection, text_embeds)


def solution(mesh):
    fine = Mesh(mesh.devices.reshape(SIZES), AXES)
    rows = P(AXES, None)
    in_specs = (rows, rows, rows, P(), P(), rows, P(), P(), P())
    return jax.shard_map(
        shards, mesh=fine, in_specs=in_specs, out_specs=(rows, rows), check_vma=False
    )
```

```python
import math

import jax
import jax.numpy as jnp
from jax import lax
from jax.experimental import pallas as pl
from jax.experimental.pallas import tpu as pltpu
from jax.sharding import Mesh, PartitionSpec as P

H = 16
HD = 96

AXES = ("y_hi", "x_hi", "x_lo", "core", "z_hi", "z_lo", "y_lo")
SIZES = (2, 2, 2, 2, 8, 4, 2)
PLANE = ("core", "y_hi", "x_hi", "y_lo", "x_lo")

BLOCK = 8
HALF = 4
LANES = 128
SPARE = (3, 7)
FILLED = (0, 1, 2, 4, 5, 6)
PARTS = 4

epsilon = 1e-06
VMEM = pl.BlockSpec(memory_space=pltpu.VMEM)
SMEM = pl.BlockSpec(memory_space=pltpu.SMEM)
HBM = pl.BlockSpec(memory_space=pltpu.HBM)
PARAMS = pltpu.CompilerParams(vmem_limit_bytes=24 << 20)


def row_norm(rows):
    return jnp.sqrt(jnp.sum(rows * rows, axis=1, keepdims=True) + epsilon)


def pack(rows):
    main = rows.shape[2] - len(SPARE) * LANES
    place = lax.broadcasted_iota(jnp.int32, (rows.shape[0], BLOCK, LANES), 1)
    runs = []
    for run in range(main // LANES):
        here = rows[:, :, run * LANES : (run + 1) * LANES]
        for step, spare in enumerate(SPARE):
            if run < len(FILLED):
                at = main + step * LANES
                moved = rows[:, FILLED[run] : FILLED[run] + 1, at : at + LANES]
                here = jnp.where(place == spare, moved, here)
            else:
                here = jnp.where(place == spare, 0.0, here)
        runs.append(here)
    return jnp.concatenate(runs, axis=2)


def unpack(rows):
    place = lax.broadcasted_iota(jnp.int32, (rows.shape[0], BLOCK, LANES), 1)
    runs = []
    for run in range(rows.shape[2] // LANES):
        here = rows[:, :, run * LANES : (run + 1) * LANES]
        for spare in SPARE:
            here = jnp.where(place == spare, 0.0, here)
        runs.append(here)
    for spare in SPARE:
        tail = jnp.zeros(place.shape, rows.dtype)
        for run, filled in enumerate(FILLED):
            moved = rows[:, spare : spare + 1, run * LANES : (run + 1) * LANES]
            tail = jnp.where(place == filled, moved, tail)
        runs.append(tail)
    return jnp.concatenate(runs, axis=2)


def unpack_rows(rows):
    wide = unpack(rows.astype(jnp.float32).reshape(-1, BLOCK, rows.shape[1]))
    return wide.reshape(-1, wide.shape[2]).astype(jnp.bfloat16)


def units_kernel(
    lengths_at,
    keys_at,
    values_at,
    probe,
    projection_at,
    text_at,
    block,
    copies,
    projected,
    lengths,
    keys,
    values,
    projection,
    text,
    pooled,
    units,
    arrived,
):
    deep = projection.shape[0] // PARTS
    fetches = [
        pltpu.make_async_copy(source, target, arrived.at[i])
        for i, (source, target) in enumerate(
            [
                (lengths_at, lengths),
                (keys_at, keys),
                (values_at, values),
                (text_at, text),
            ]
            + [
                (projection_at.at[pl.ds(part * deep, deep)], projection.at[pl.ds(part * deep, deep)])
                for part in range(PARTS)
            ]
        )
    ]
    for fetch in fetches:
        fetch.start()
    n_rows, width = keys.shape
    head = lax.broadcasted_iota(jnp.int32, (H, width), 0)
    own = lax.broadcasted_iota(jnp.int32, (H, width), 1) // HD == head
    query = jnp.where(own, probe[...].astype(jnp.float32).reshape(1, width), 0.0).astype(jnp.bfloat16)
    fetches[0].wait()
    fetches[1].wait()
    scores = lax.dot_general(
        query, keys[...], (((1,), (1,)), ((), ())), preferred_element_type=jnp.float32
    ) / math.sqrt(HD)
    row = lax.broadcasted_iota(jnp.int32, (H, n_rows), 1)
    start = jnp.int32(0)
    weights = []
    for image in range(lengths.shape[1]):
        end = start + lengths[0, image]
        member = (row >= start) & (row < end)
        masked = jnp.where(member, scores, -jnp.inf)
        terms = jnp.exp(masked - jnp.max(masked, axis=1, keepdims=True))
        weights.append((terms / jnp.sum(terms, axis=1, keepdims=True)).astype(jnp.bfloat16))
        start = end
    fetches[2].wait()
    mixed = jnp.dot(
        jnp.concatenate(weights), values[...], preferred_element_type=jnp.float32
    )
    pooled[...] = jnp.zeros_like(pooled)
    for image in range(lengths.shape[1]):
        part = mixed[image * H : (image + 1) * H]
        pooled[image : image + 1, :] = jnp.sum(jnp.where(own, part, 0.0), axis=0, keepdims=True)
    proj = jnp.zeros((2 * BLOCK, projected.shape[1]), jnp.float32)
    for part in range(PARTS):
        fetches[4 + part].wait()
        here = slice(part * deep, (part + 1) * deep)
        proj += jnp.dot(
            pooled[:, here].astype(jnp.bfloat16),
            projection[here, :],
            preferred_element_type=jnp.float32,
        )
    proj = proj[:BLOCK]
    fetches[3].wait()
    projected[...] = proj
    units[...] = proj / row_norm(proj)
    text_wide = text[...].astype(jnp.float32)
    count = text.shape[0]
    units[HALF : HALF + count, :] = text_wide / row_norm(text_wide)
    packed = pack(units[...][None])
    block[...] = packed[0].astype(jnp.bfloat16)
    n = copies.shape[0] // BLOCK
    copies[...] = (
        jnp.broadcast_to(packed, (n,) + packed.shape[1:]).reshape(copies.shape).astype(jnp.bfloat16)
    )


def pick(groups, positions, axis):
    n_rows, lanes = groups.shape
    n = positions.shape[axis]
    high, low = groups // 64, groups % 64
    pieces = []
    for digit in (high, low):
        digit = digit.astype(jnp.float32).astype(jnp.bfloat16)
        if axis == 0:
            lane = lax.broadcasted_iota(jnp.int32, (n, lanes), 1)
            hot = jnp.where(lane == positions % lanes, 1.0, 0.0).astype(jnp.bfloat16)
            found = lax.dot_general(
                hot, digit, (((1,), (1,)), ((), ())), preferred_element_type=jnp.float32
            )
            line = lax.broadcasted_iota(jnp.int32, (n, n_rows), 1)
        else:
            lane = lax.broadcasted_iota(jnp.int32, (lanes, n), 0)
            hot = jnp.where(lane == positions % lanes, 1.0, 0.0).astype(jnp.bfloat16)
            found = jnp.dot(digit, hot, preferred_element_type=jnp.float32)
            line = lax.broadcasted_iota(jnp.int32, (n_rows, n), 0)
        kept = jnp.where(line == positions // lanes, found, 0.0)
        pieces.append(jnp.sum(kept, axis=1 - axis, keepdims=True))
    return pieces[0] * 64.0 + pieces[1]


def device(place, sizes):
    number = 0
    for axis in AXES:
        number = number * sizes[axis] + place[axis]
    return number


def tile_kernel(count, plane, *refs):
    *lines, groups, scale, bias, parts = refs
    line = jnp.concatenate([unpack_rows(rows[...]) for rows in lines])
    sizes = dict((axis, lax.axis_size(axis)) for axis in AXES)
    place = dict((axis, lax.axis_index(axis)) for axis in AXES)
    at = lax.broadcasted_iota(jnp.int32, (plane.shape[0], 1), 0)
    member, slot = at // BLOCK, jnp.minimum(at % HALF, count - 1)
    there = dict(place)
    for axis in PLANE[::-1]:
        there[axis] = member % sizes[axis]
        member = member // sizes[axis]
    plane_at = device(there, sizes) * count + slot
    plane_kind = at % BLOCK // HALF
    at = lax.broadcasted_iota(jnp.int32, (1, line.shape[0]), 1)
    member, slot = at // BLOCK, jnp.minimum(at % HALF, count - 1)
    behind = place["z_lo"] - member // sizes["z_hi"] + sizes["z_lo"]
    there = dict(place, z_hi=member % sizes["z_hi"], z_lo=behind % sizes["z_lo"])
    line_at = device(there, sizes) * count + slot
    line_kind = at % BLOCK // HALF
    plane_ids = pick(groups[...], plane_at, 0)
    line_ids = pick(groups[...], line_at, 1)

    plane_rows = unpack_rows(plane[...])
    logits = (
        lax.dot_general(
            plane_rows, line, (((1,), (1,)), ((), ())), preferred_element_type=jnp.float32
        )
        * scale[0]
        + bias[0]
    )
    labels = jnp.where(plane_ids == line_ids, 1.0, -1.0)
    coeffs = -labels * jax.nn.sigmoid(-labels * logits) * scale[0]
    coeffs = jnp.where(plane_kind != line_kind, coeffs, 0.0).astype(jnp.bfloat16)
    wide = jnp.dot(coeffs, line, preferred_element_type=jnp.float32)
    packed = pack(wide.reshape(-1, BLOCK, wide.shape[1]))
    parts[...] = packed.reshape(parts.shape).astype(jnp.bfloat16)


def grads_kernel(parts, projected, projection, text, pooled_grad, text_grad, sums):
    count, width = text.shape
    total = parts[...].astype(jnp.float32).reshape(-1, BLOCK, parts.shape[1])
    total = unpack(jnp.sum(total, axis=0, keepdims=True))[0]
    sums[...] = total
    proj = projected[...]
    norm = row_norm(proj)
    u = proj / norm
    d_proj = (total - jnp.sum(total * u, axis=1, keepdims=True) * u) / norm
    d_proj = jnp.concatenate([d_proj, jnp.zeros_like(d_proj)]).astype(jnp.bfloat16)
    pooled_grad[...] = lax.dot_general(
        d_proj, projection[...], (((1,), (1,)), ((), ())), preferred_element_type=jnp.float32
    )[:count]
    text_wide = text[...].astype(jnp.float32)
    norm = row_norm(text_wide)
    v = text_wide / norm
    d_txt = sums[HALF : HALF + count, :]
    text_grad[...] = (d_txt - jnp.sum(d_txt * v, axis=1, keepdims=True) * v) / norm


def exchange(rows, axis):
    shape = (lax.axis_size(axis), -1, rows.shape[1])
    return lax.all_to_all(rows.reshape(shape), axis, 0, 0, tiled=True).reshape(rows.shape)


def shards(
    patch_keys,
    patch_values,
    lengths,
    probe_query,
    projection,
    text_embeds,
    pair_group,
    logit_scale,
    logit_bias,
):
    count, width = text_embeds.shape
    depth = patch_keys.shape[1]
    n_far = lax.axis_size("z_hi")
    n_plane = lax.axis_size(PLANE)
    narrow = width - len(SPARE) * LANES
    block, copies, projected = pl.pallas_call(
        units_kernel,
        out_shape=(
            jax.ShapeDtypeStruct((BLOCK, narrow), jnp.bfloat16),
            jax.ShapeDtypeStruct((n_far * BLOCK, narrow), jnp.bfloat16),
            jax.ShapeDtypeStruct((BLOCK, width), jnp.float32),
        ),
        in_specs=[HBM] * 3 + [VMEM] + [HBM] * 2,
        out_specs=(VMEM, VMEM, VMEM),
        scratch_shapes=[
            pltpu.SMEM(lengths.shape, lengths.dtype),
            pltpu.VMEM(patch_keys.shape, patch_keys.dtype),
            pltpu.VMEM(patch_values.shape, patch_values.dtype),
            pltpu.VMEM(projection.shape, projection.dtype),
            pltpu.VMEM(text_embeds.shape, text_embeds.dtype),
            pltpu.VMEM((2 * BLOCK, depth), jnp.float32),
            pltpu.VMEM((BLOCK, width), jnp.float32),
            pltpu.SemaphoreType.DMA((4 + PARTS,)),
        ],
        compiler_params=pltpu.CompilerParams(vmem_limit_bytes=60 << 20),
        name="units",
    )(lengths, patch_keys, patch_values, probe_query, projection, text_embeds)

    far = exchange(copies, "z_hi")
    plane = block
    for axis in PLANE[:0:-1]:
        plane = lax.all_gather(plane, axis, axis=0, tiled=True)
    far, plane = lax.optimization_barrier((far, plane))
    plane = lax.all_gather(plane, PLANE[0], axis=0, tiled=True)
    n_near = lax.axis_size("z_lo")
    lines = [far]
    for ahead in range(1, n_near):
        route = [(i, (i + ahead) % n_near) for i in range(n_near)]
        lines.append(lax.ppermute(far, "z_lo", route))
    parts = pl.pallas_call(
        lambda *refs: tile_kernel(count, *refs),
        out_shape=jax.ShapeDtypeStruct((n_plane * BLOCK, narrow), jnp.bfloat16),
        in_specs=[VMEM] * (2 + n_near) + [SMEM] * 2,
        out_specs=VMEM,
        compiler_params=PARAMS,
        name="tile",
    )(
        plane,
        *lines,
        pair_group.reshape(-1, 128),
        logit_scale,
        logit_bias,
    )
    parts = exchange(parts, PLANE)
    return pl.pallas_call(
        grads_kernel,
        out_shape=(
            jax.ShapeDtypeStruct((count, depth), jnp.float32),
            jax.ShapeDtypeStruct((count, width), jnp.float32),
        ),
        in_specs=[VMEM] * 4,
        out_specs=(VMEM, VMEM),
        scratch_shapes=[pltpu.VMEM((BLOCK, width), jnp.float32)],
        compiler_params=PARAMS,
        name="grads",
    )(parts, projected, projection, text_embeds)


def solution(mesh):
    fine = Mesh(mesh.devices.reshape(SIZES), AXES)
    rows = P(AXES, None)
    in_specs = (rows, rows, rows, P(), P(), rows, P(), P(), P())
    return jax.shard_map(
        shards, mesh=fine, in_specs=in_specs, out_specs=(rows, rows), check_vma=False
    )
```

```python
import math

import jax
import jax.numpy as jnp
from jax import lax
from jax.experimental import pallas as pl
from jax.experimental.pallas import tpu as pltpu
from jax.sharding import Mesh, PartitionSpec as P

H = 16
HD = 96

AXES = ("y_hi", "x_hi", "x_lo", "core", "z_hi", "z_lo", "y_lo")
SIZES = (2, 2, 2, 2, 16, 2, 2)
PLANE = ("core", "y_hi", "x_hi", "y_lo", "x_lo")

BLOCK = 8
HALF = 4
LANES = 128
SPARE = (3, 7)
FILLED = (0, 1, 2, 4, 5, 6)
PARTS = 4

epsilon = 1e-06
VMEM = pl.BlockSpec(memory_space=pltpu.VMEM)
SMEM = pl.BlockSpec(memory_space=pltpu.SMEM)
HBM = pl.BlockSpec(memory_space=pltpu.HBM)
PARAMS = pltpu.CompilerParams(vmem_limit_bytes=24 << 20)


def row_norm(rows):
    return jnp.sqrt(jnp.sum(rows * rows, axis=1, keepdims=True) + epsilon)


def pack(rows):
    main = rows.shape[2] - len(SPARE) * LANES
    place = lax.broadcasted_iota(jnp.int32, (rows.shape[0], BLOCK, LANES), 1)
    runs = []
    for run in range(main // LANES):
        here = rows[:, :, run * LANES : (run + 1) * LANES]
        for step, spare in enumerate(SPARE):
            if run < len(FILLED):
                at = main + step * LANES
                moved = rows[:, FILLED[run] : FILLED[run] + 1, at : at + LANES]
                here = jnp.where(place == spare, moved, here)
            else:
                here = jnp.where(place == spare, 0.0, here)
        runs.append(here)
    return jnp.concatenate(runs, axis=2)


def unpack(rows):
    place = lax.broadcasted_iota(jnp.int32, (rows.shape[0], BLOCK, LANES), 1)
    runs = []
    for run in range(rows.shape[2] // LANES):
        here = rows[:, :, run * LANES : (run + 1) * LANES]
        for spare in SPARE:
            here = jnp.where(place == spare, 0.0, here)
        runs.append(here)
    for spare in SPARE:
        tail = jnp.zeros(place.shape, rows.dtype)
        for run, filled in enumerate(FILLED):
            moved = rows[:, spare : spare + 1, run * LANES : (run + 1) * LANES]
            tail = jnp.where(place == filled, moved, tail)
        runs.append(tail)
    return jnp.concatenate(runs, axis=2)


def unpack_rows(rows):
    wide = unpack(rows.astype(jnp.float32).reshape(-1, BLOCK, rows.shape[1]))
    return wide.reshape(-1, wide.shape[2]).astype(jnp.bfloat16)


def units_kernel(
    lengths_at,
    keys_at,
    values_at,
    probe,
    projection_at,
    text_at,
    block,
    copies,
    projected,
    lengths,
    keys,
    values,
    projection,
    text,
    pooled,
    units,
    arrived,
):
    deep = projection.shape[0] // PARTS
    fetches = [
        pltpu.make_async_copy(source, target, arrived.at[i])
        for i, (source, target) in enumerate(
            [
                (lengths_at, lengths),
                (keys_at, keys),
                (values_at, values),
                (text_at, text),
            ]
            + [
                (projection_at.at[pl.ds(part * deep, deep)], projection.at[pl.ds(part * deep, deep)])
                for part in range(PARTS)
            ]
        )
    ]
    for fetch in fetches:
        fetch.start()
    n_rows, width = keys.shape
    head = lax.broadcasted_iota(jnp.int32, (H, width), 0)
    own = lax.broadcasted_iota(jnp.int32, (H, width), 1) // HD == head
    query = jnp.where(own, probe[...].astype(jnp.float32).reshape(1, width), 0.0).astype(jnp.bfloat16)
    fetches[0].wait()
    fetches[1].wait()
    scores = lax.dot_general(
        query, keys[...], (((1,), (1,)), ((), ())), preferred_element_type=jnp.float32
    ) / math.sqrt(HD)
    row = lax.broadcasted_iota(jnp.int32, (H, n_rows), 1)
    start = jnp.int32(0)
    weights = []
    for image in range(lengths.shape[1]):
        end = start + lengths[0, image]
        member = (row >= start) & (row < end)
        masked = jnp.where(member, scores, -jnp.inf)
        terms = jnp.exp(masked - jnp.max(masked, axis=1, keepdims=True))
        weights.append((terms / jnp.sum(terms, axis=1, keepdims=True)).astype(jnp.bfloat16))
        start = end
    fetches[2].wait()
    mixed = jnp.dot(
        jnp.concatenate(weights), values[...], preferred_element_type=jnp.float32
    )
    pooled[...] = jnp.zeros_like(pooled)
    for image in range(lengths.shape[1]):
        part = mixed[image * H : (image + 1) * H]
        pooled[image : image + 1, :] = jnp.sum(jnp.where(own, part, 0.0), axis=0, keepdims=True)
    proj = jnp.zeros((2 * BLOCK, projected.shape[1]), jnp.float32)
    for part in range(PARTS):
        fetches[4 + part].wait()
        here = slice(part * deep, (part + 1) * deep)
        proj += jnp.dot(
            pooled[:, here].astype(jnp.bfloat16),
            projection[here, :],
            preferred_element_type=jnp.float32,
        )
    proj = proj[:BLOCK]
    fetches[3].wait()
    projected[...] = proj
    units[...] = proj / row_norm(proj)
    text_wide = text[...].astype(jnp.float32)
    count = text.shape[0]
    units[HALF : HALF + count, :] = text_wide / row_norm(text_wide)
    packed = pack(units[...][None])
    block[...] = packed[0].astype(jnp.bfloat16)
    n = copies.shape[0] // BLOCK
    copies[...] = (
        jnp.broadcast_to(packed, (n,) + packed.shape[1:]).reshape(copies.shape).astype(jnp.bfloat16)
    )


def pick(groups, positions, axis):
    n_rows, lanes = groups.shape
    n = positions.shape[axis]
    high, low = groups // 64, groups % 64
    pieces = []
    for digit in (high, low):
        digit = digit.astype(jnp.float32).astype(jnp.bfloat16)
        if axis == 0:
            lane = lax.broadcasted_iota(jnp.int32, (n, lanes), 1)
            hot = jnp.where(lane == positions % lanes, 1.0, 0.0).astype(jnp.bfloat16)
            found = lax.dot_general(
                hot, digit, (((1,), (1,)), ((), ())), preferred_element_type=jnp.float32
            )
            line = lax.broadcasted_iota(jnp.int32, (n, n_rows), 1)
        else:
            lane = lax.broadcasted_iota(jnp.int32, (lanes, n), 0)
            hot = jnp.where(lane == positions % lanes, 1.0, 0.0).astype(jnp.bfloat16)
            found = jnp.dot(digit, hot, preferred_element_type=jnp.float32)
            line = lax.broadcasted_iota(jnp.int32, (n_rows, n), 0)
        kept = jnp.where(line == positions // lanes, found, 0.0)
        pieces.append(jnp.sum(kept, axis=1 - axis, keepdims=True))
    return pieces[0] * 64.0 + pieces[1]


def device(place, sizes):
    number = 0
    for axis in AXES:
        number = number * sizes[axis] + place[axis]
    return number


def tile_kernel(count, plane, *refs):
    *lines, groups, scale, bias, parts = refs
    line = jnp.concatenate([unpack_rows(rows[...]) for rows in lines])
    sizes = dict((axis, lax.axis_size(axis)) for axis in AXES)
    place = dict((axis, lax.axis_index(axis)) for axis in AXES)
    at = lax.broadcasted_iota(jnp.int32, (plane.shape[0], 1), 0)
    member, slot = at // BLOCK, jnp.minimum(at % HALF, count - 1)
    there = dict(place)
    for axis in PLANE[::-1]:
        there[axis] = member % sizes[axis]
        member = member // sizes[axis]
    plane_at = device(there, sizes) * count + slot
    plane_kind = at % BLOCK // HALF
    at = lax.broadcasted_iota(jnp.int32, (1, line.shape[0]), 1)
    member, slot = at // BLOCK, jnp.minimum(at % HALF, count - 1)
    behind = place["z_lo"] - member // sizes["z_hi"] + sizes["z_lo"]
    there = dict(place, z_hi=member % sizes["z_hi"], z_lo=behind % sizes["z_lo"])
    line_at = device(there, sizes) * count + slot
    line_kind = at % BLOCK // HALF
    plane_ids = pick(groups[...], plane_at, 0)
    line_ids = pick(groups[...], line_at, 1)

    plane_rows = unpack_rows(plane[...])
    logits = (
        lax.dot_general(
            plane_rows, line, (((1,), (1,)), ((), ())), preferred_element_type=jnp.float32
        )
        * scale[0]
        + bias[0]
    )
    labels = jnp.where(plane_ids == line_ids, 1.0, -1.0)
    coeffs = -labels * jax.nn.sigmoid(-labels * logits) * scale[0]
    coeffs = jnp.where(plane_kind != line_kind, coeffs, 0.0).astype(jnp.bfloat16)
    wide = jnp.dot(coeffs, line, preferred_element_type=jnp.float32)
    packed = pack(wide.reshape(-1, BLOCK, wide.shape[1]))
    parts[...] = packed.reshape(parts.shape).astype(jnp.bfloat16)


def grads_kernel(parts, projected, projection, text, pooled_grad, text_grad, sums):
    count, width = text.shape
    total = parts[...].astype(jnp.float32).reshape(-1, BLOCK, parts.shape[1])
    total = unpack(jnp.sum(total, axis=0, keepdims=True))[0]
    sums[...] = total
    proj = projected[...]
    norm = row_norm(proj)
    u = proj / norm
    d_proj = (total - jnp.sum(total * u, axis=1, keepdims=True) * u) / norm
    d_proj = jnp.concatenate([d_proj, jnp.zeros_like(d_proj)]).astype(jnp.bfloat16)
    pooled_grad[...] = lax.dot_general(
        d_proj, projection[...], (((1,), (1,)), ((), ())), preferred_element_type=jnp.float32
    )[:count]
    text_wide = text[...].astype(jnp.float32)
    norm = row_norm(text_wide)
    v = text_wide / norm
    d_txt = sums[HALF : HALF + count, :]
    text_grad[...] = (d_txt - jnp.sum(d_txt * v, axis=1, keepdims=True) * v) / norm


def exchange(rows, axis):
    shape = (lax.axis_size(axis), -1, rows.shape[1])
    return lax.all_to_all(rows.reshape(shape), axis, 0, 0, tiled=True).reshape(rows.shape)


def shards(
    patch_keys,
    patch_values,
    lengths,
    probe_query,
    projection,
    text_embeds,
    pair_group,
    logit_scale,
    logit_bias,
):
    count, width = text_embeds.shape
    depth = patch_keys.shape[1]
    n_far = lax.axis_size("z_hi")
    n_plane = lax.axis_size(PLANE)
    narrow = width - len(SPARE) * LANES
    block, copies, projected = pl.pallas_call(
        units_kernel,
        out_shape=(
            jax.ShapeDtypeStruct((BLOCK, narrow), jnp.bfloat16),
            jax.ShapeDtypeStruct((n_far * BLOCK, narrow), jnp.bfloat16),
            jax.ShapeDtypeStruct((BLOCK, width), jnp.float32),
        ),
        in_specs=[HBM] * 3 + [VMEM] + [HBM] * 2,
        out_specs=(VMEM, VMEM, VMEM),
        scratch_shapes=[
            pltpu.SMEM(lengths.shape, lengths.dtype),
            pltpu.VMEM(patch_keys.shape, patch_keys.dtype),
            pltpu.VMEM(patch_values.shape, patch_values.dtype),
            pltpu.VMEM(projection.shape, projection.dtype),
            pltpu.VMEM(text_embeds.shape, text_embeds.dtype),
            pltpu.VMEM((2 * BLOCK, depth), jnp.float32),
            pltpu.VMEM((BLOCK, width), jnp.float32),
            pltpu.SemaphoreType.DMA((4 + PARTS,)),
        ],
        compiler_params=pltpu.CompilerParams(vmem_limit_bytes=60 << 20),
        name="units",
    )(lengths, patch_keys, patch_values, probe_query, projection, text_embeds)

    far = exchange(copies, "z_hi")
    plane = block
    for axis in PLANE[:0:-1]:
        plane = lax.all_gather(plane, axis, axis=0, tiled=True)
    far, plane = lax.optimization_barrier((far, plane))
    plane = lax.all_gather(plane, PLANE[0], axis=0, tiled=True)
    n_near = lax.axis_size("z_lo")
    lines = [far]
    for ahead in range(1, n_near):
        route = [(i, (i + ahead) % n_near) for i in range(n_near)]
        lines.append(lax.ppermute(far, "z_lo", route))
    parts = pl.pallas_call(
        lambda *refs: tile_kernel(count, *refs),
        out_shape=jax.ShapeDtypeStruct((n_plane * BLOCK, narrow), jnp.bfloat16),
        in_specs=[VMEM] * (2 + n_near) + [SMEM] * 2,
        out_specs=VMEM,
        compiler_params=PARAMS,
        name="tile",
    )(
        plane,
        *lines,
        pair_group.reshape(-1, 128),
        logit_scale,
        logit_bias,
    )
    parts = exchange(parts, PLANE)
    return pl.pallas_call(
        grads_kernel,
        out_shape=(
            jax.ShapeDtypeStruct((count, depth), jnp.float32),
            jax.ShapeDtypeStruct((count, width), jnp.float32),
        ),
        in_specs=[VMEM] * 4,
        out_specs=(VMEM, VMEM),
        scratch_shapes=[pltpu.VMEM((BLOCK, width), jnp.float32)],
        compiler_params=PARAMS,
        name="grads",
    )(parts, projected, projection, text_embeds)


def solution(mesh):
    fine = Mesh(mesh.devices.reshape(SIZES), AXES)
    rows = P(AXES, None)
    in_specs = (rows, rows, rows, P(), P(), rows, P(), P(), P())
    return jax.shard_map(
        shards, mesh=fine, in_specs=in_specs, out_specs=(rows, rows), check_vma=False
    )
```

```python
import math

import jax
import jax.numpy as jnp
from jax import lax
from jax.experimental import pallas as pl
from jax.experimental.pallas import tpu as pltpu
from jax.sharding import Mesh, PartitionSpec as P

H = 16
HD = 96

AXES = ("y_hi", "x_hi", "x_lo", "core", "z_hi", "z_lo", "y_lo")
SIZES = (2, 2, 2, 2, 16, 2, 2)
PLANE = ("core", "y_hi", "x_hi", "y_lo", "x_lo")

BLOCK = 8
HALF = 4
LANES = 128
SPARE = (3, 7)
FILLED = (0, 1, 2, 4, 5, 6)
PARTS = 4

epsilon = 1e-06
VMEM = pl.BlockSpec(memory_space=pltpu.VMEM)
SMEM = pl.BlockSpec(memory_space=pltpu.SMEM)
HBM = pl.BlockSpec(memory_space=pltpu.HBM)
PARAMS = pltpu.CompilerParams(vmem_limit_bytes=24 << 20)


def row_norm(rows):
    return jnp.sqrt(jnp.sum(rows * rows, axis=1, keepdims=True) + epsilon)


def pack(rows):
    main = rows.shape[2] - len(SPARE) * LANES
    place = lax.broadcasted_iota(jnp.int32, (rows.shape[0], BLOCK, LANES), 1)
    runs = []
    for run in range(main // LANES):
        here = rows[:, :, run * LANES : (run + 1) * LANES]
        for step, spare in enumerate(SPARE):
            if run < len(FILLED):
                at = main + step * LANES
                moved = rows[:, FILLED[run] : FILLED[run] + 1, at : at + LANES]
                here = jnp.where(place == spare, moved, here)
            else:
                here = jnp.where(place == spare, 0.0, here)
        runs.append(here)
    return jnp.concatenate(runs, axis=2)


def unpack(rows):
    place = lax.broadcasted_iota(jnp.int32, (rows.shape[0], BLOCK, LANES), 1)
    runs = []
    for run in range(rows.shape[2] // LANES):
        here = rows[:, :, run * LANES : (run + 1) * LANES]
        for spare in SPARE:
            here = jnp.where(place == spare, 0.0, here)
        runs.append(here)
    for spare in SPARE:
        tail = jnp.zeros(place.shape, rows.dtype)
        for run, filled in enumerate(FILLED):
            moved = rows[:, spare : spare + 1, run * LANES : (run + 1) * LANES]
            tail = jnp.where(place == filled, moved, tail)
        runs.append(tail)
    return jnp.concatenate(runs, axis=2)


def unpack_rows(rows):
    wide = unpack(rows.astype(jnp.float32).reshape(-1, BLOCK, rows.shape[1]))
    return wide.reshape(-1, wide.shape[2]).astype(jnp.bfloat16)


def units_kernel(
    lengths_at,
    keys_at,
    values_at,
    probe,
    projection_at,
    text,
    block,
    copies,
    projected,
    lengths,
    keys,
    values,
    projection,
    pooled,
    units,
    arrived,
):
    deep = projection.shape[0] // PARTS
    fetches = [
        pltpu.make_async_copy(source, target, arrived.at[i])
        for i, (source, target) in enumerate(
            [
                (lengths_at, lengths),
                (keys_at, keys),
                (values_at, values),
            ]
            + [
                (projection_at.at[pl.ds(part * deep, deep)], projection.at[pl.ds(part * deep, deep)])
                for part in range(PARTS)
            ]
        )
    ]
    for fetch in fetches:
        fetch.start()
    n_rows, width = keys.shape
    head = lax.broadcasted_iota(jnp.int32, (H, width), 0)
    own = lax.broadcasted_iota(jnp.int32, (H, width), 1) // HD == head
    query = jnp.where(own, probe[...].astype(jnp.float32).reshape(1, width), 0.0).astype(jnp.bfloat16)
    fetches[0].wait()
    fetches[1].wait()
    scores = lax.dot_general(
        query, keys[...], (((1,), (1,)), ((), ())), preferred_element_type=jnp.float32
    ) / math.sqrt(HD)
    row = lax.broadcasted_iota(jnp.int32, (H, n_rows), 1)
    start = jnp.int32(0)
    weights = []
    for image in range(lengths.shape[1]):
        end = start + lengths[0, image]
        member = (row >= start) & (row < end)
        masked = jnp.where(member, scores, -jnp.inf)
        terms = jnp.exp(masked - jnp.max(masked, axis=1, keepdims=True))
        weights.append((terms / jnp.sum(terms, axis=1, keepdims=True)).astype(jnp.bfloat16))
        start = end
    fetches[2].wait()
    mixed = jnp.dot(
        jnp.concatenate(weights), values[...], preferred_element_type=jnp.float32
    )
    pooled[...] = jnp.zeros_like(pooled)
    for image in range(lengths.shape[1]):
        part = mixed[image * H : (image + 1) * H]
        pooled[image : image + 1, :] = jnp.sum(jnp.where(own, part, 0.0), axis=0, keepdims=True)
    proj = jnp.zeros((2 * BLOCK, projected.shape[1]), jnp.float32)
    for part in range(PARTS):
        fetches[3 + part].wait()
        here = slice(part * deep, (part + 1) * deep)
        proj += jnp.dot(
            pooled[:, here].astype(jnp.bfloat16),
            projection[here, :],
            preferred_element_type=jnp.float32,
        )
    proj = proj[:BLOCK]
    projected[...] = proj
    units[...] = proj / row_norm(proj)
    text_wide = text[...].astype(jnp.float32)
    count = text.shape[0]
    units[HALF : HALF + count, :] = text_wide / row_norm(text_wide)
    packed = pack(units[...][None])
    block[...] = packed[0].astype(jnp.bfloat16)
    n = copies.shape[0] // BLOCK
    copies[...] = (
        jnp.broadcast_to(packed, (n,) + packed.shape[1:]).reshape(copies.shape).astype(jnp.bfloat16)
    )


def pick(groups, positions, axis):
    n_rows, lanes = groups.shape
    n = positions.shape[axis]
    high, low = groups // 64, groups % 64
    pieces = []
    for digit in (high, low):
        digit = digit.astype(jnp.float32).astype(jnp.bfloat16)
        if axis == 0:
            lane = lax.broadcasted_iota(jnp.int32, (n, lanes), 1)
            hot = jnp.where(lane == positions % lanes, 1.0, 0.0).astype(jnp.bfloat16)
            found = lax.dot_general(
                hot, digit, (((1,), (1,)), ((), ())), preferred_element_type=jnp.float32
            )
            line = lax.broadcasted_iota(jnp.int32, (n, n_rows), 1)
        else:
            lane = lax.broadcasted_iota(jnp.int32, (lanes, n), 0)
            hot = jnp.where(lane == positions % lanes, 1.0, 0.0).astype(jnp.bfloat16)
            found = jnp.dot(digit, hot, preferred_element_type=jnp.float32)
            line = lax.broadcasted_iota(jnp.int32, (n_rows, n), 0)
        kept = jnp.where(line == positions // lanes, found, 0.0)
        pieces.append(jnp.sum(kept, axis=1 - axis, keepdims=True))
    return pieces[0] * 64.0 + pieces[1]


def device(place, sizes):
    number = 0
    for axis in AXES:
        number = number * sizes[axis] + place[axis]
    return number


def tile_kernel(count, plane, *refs):
    *lines, groups, scale, bias, parts = refs
    line = jnp.concatenate([unpack_rows(rows[...]) for rows in lines])
    sizes = dict((axis, lax.axis_size(axis)) for axis in AXES)
    place = dict((axis, lax.axis_index(axis)) for axis in AXES)
    at = lax.broadcasted_iota(jnp.int32, (plane.shape[0], 1), 0)
    member, slot = at // BLOCK, jnp.minimum(at % HALF, count - 1)
    there = dict(place)
    for axis in PLANE[::-1]:
        there[axis] = member % sizes[axis]
        member = member // sizes[axis]
    plane_at = device(there, sizes) * count + slot
    plane_kind = at % BLOCK // HALF
    at = lax.broadcasted_iota(jnp.int32, (1, line.shape[0]), 1)
    member, slot = at // BLOCK, jnp.minimum(at % HALF, count - 1)
    behind = place["z_lo"] - member // sizes["z_hi"] + sizes["z_lo"]
    there = dict(place, z_hi=member % sizes["z_hi"], z_lo=behind % sizes["z_lo"])
    line_at = device(there, sizes) * count + slot
    line_kind = at % BLOCK // HALF
    plane_ids = pick(groups[...], plane_at, 0)
    line_ids = pick(groups[...], line_at, 1)

    plane_rows = unpack_rows(plane[...])
    logits = (
        lax.dot_general(
            plane_rows, line, (((1,), (1,)), ((), ())), preferred_element_type=jnp.float32
        )
        * scale[0]
        + bias[0]
    )
    labels = jnp.where(plane_ids == line_ids, 1.0, -1.0)
    coeffs = -labels * jax.nn.sigmoid(-labels * logits) * scale[0]
    coeffs = jnp.where(plane_kind != line_kind, coeffs, 0.0).astype(jnp.bfloat16)
    wide = jnp.dot(coeffs, line, preferred_element_type=jnp.float32)
    packed = pack(wide.reshape(-1, BLOCK, wide.shape[1]))
    parts[...] = packed.reshape(parts.shape).astype(jnp.bfloat16)


def grads_kernel(parts, projected, projection, text, pooled_grad, text_grad, sums):
    count, width = text.shape
    total = parts[...].astype(jnp.float32).reshape(-1, BLOCK, parts.shape[1])
    total = unpack(jnp.sum(total, axis=0, keepdims=True))[0]
    sums[...] = total
    proj = projected[...]
    norm = row_norm(proj)
    u = proj / norm
    d_proj = (total - jnp.sum(total * u, axis=1, keepdims=True) * u) / norm
    d_proj = jnp.concatenate([d_proj, jnp.zeros_like(d_proj)]).astype(jnp.bfloat16)
    pooled_grad[...] = lax.dot_general(
        d_proj, projection[...], (((1,), (1,)), ((), ())), preferred_element_type=jnp.float32
    )[:count]
    text_wide = text[...].astype(jnp.float32)
    norm = row_norm(text_wide)
    v = text_wide / norm
    d_txt = sums[HALF : HALF + count, :]
    text_grad[...] = (d_txt - jnp.sum(d_txt * v, axis=1, keepdims=True) * v) / norm


def exchange(rows, axis):
    shape = (lax.axis_size(axis), -1, rows.shape[1])
    return lax.all_to_all(rows.reshape(shape), axis, 0, 0, tiled=True).reshape(rows.shape)


def shards(
    patch_keys,
    patch_values,
    lengths,
    probe_query,
    projection,
    text_embeds,
    pair_group,
    logit_scale,
    logit_bias,
):
    count, width = text_embeds.shape
    depth = patch_keys.shape[1]
    n_far = lax.axis_size("z_hi")
    n_plane = lax.axis_size(PLANE)
    narrow = width - len(SPARE) * LANES
    block, copies, projected = pl.pallas_call(
        units_kernel,
        out_shape=(
            jax.ShapeDtypeStruct((BLOCK, narrow), jnp.bfloat16),
            jax.ShapeDtypeStruct((n_far * BLOCK, narrow), jnp.bfloat16),
            jax.ShapeDtypeStruct((BLOCK, width), jnp.float32),
        ),
        in_specs=[HBM] * 3 + [VMEM, HBM, VMEM],
        out_specs=(VMEM, VMEM, VMEM),
        scratch_shapes=[
            pltpu.SMEM(lengths.shape, lengths.dtype),
            pltpu.VMEM(patch_keys.shape, patch_keys.dtype),
            pltpu.VMEM(patch_values.shape, patch_values.dtype),
            pltpu.VMEM(projection.shape, projection.dtype),
            pltpu.VMEM((2 * BLOCK, depth), jnp.float32),
            pltpu.VMEM((BLOCK, width), jnp.float32),
            pltpu.SemaphoreType.DMA((3 + PARTS,)),
        ],
        compiler_params=pltpu.CompilerParams(vmem_limit_bytes=60 << 20),
        name="units",
    )(lengths, patch_keys, patch_values, probe_query, projection, text_embeds)

    far = exchange(copies, "z_hi")
    plane = block
    for axis in PLANE[:0:-1]:
        plane = lax.all_gather(plane, axis, axis=0, tiled=True)
    far, plane = lax.optimization_barrier((far, plane))
    plane = lax.all_gather(plane, PLANE[0], axis=0, tiled=True)
    n_near = lax.axis_size("z_lo")
    lines = [far]
    for ahead in range(1, n_near):
        route = [(i, (i + ahead) % n_near) for i in range(n_near)]
        lines.append(lax.ppermute(far, "z_lo", route))
    parts = pl.pallas_call(
        lambda *refs: tile_kernel(count, *refs),
        out_shape=jax.ShapeDtypeStruct((n_plane * BLOCK, narrow), jnp.bfloat16),
        in_specs=[VMEM] * (2 + n_near) + [SMEM] * 2,
        out_specs=VMEM,
        compiler_params=PARAMS,
        name="tile",
    )(
        plane,
        *lines,
        pair_group.reshape(-1, 128),
        logit_scale,
        logit_bias,
    )
    parts = exchange(parts, PLANE)
    return pl.pallas_call(
        grads_kernel,
        out_shape=(
            jax.ShapeDtypeStruct((count, depth), jnp.float32),
            jax.ShapeDtypeStruct((count, width), jnp.float32),
        ),
        in_specs=[VMEM] * 4,
        out_specs=(VMEM, VMEM),
        scratch_shapes=[pltpu.VMEM((BLOCK, width), jnp.float32)],
        compiler_params=PARAMS,
        name="grads",
    )(parts, projected, projection, text_embeds)


def solution(mesh):
    fine = Mesh(mesh.devices.reshape(SIZES), AXES)
    rows = P(AXES, None)
    in_specs = (rows, rows, rows, P(), P(), rows, P(), P(), P())
    return jax.shard_map(
        shards, mesh=fine, in_specs=in_specs, out_specs=(rows, rows), check_vma=False
    )
```

```python
import math

import jax
import jax.numpy as jnp
from jax import lax
from jax.experimental import pallas as pl
from jax.experimental.pallas import tpu as pltpu
from jax.sharding import Mesh, PartitionSpec as P

H = 16
HD = 96

AXES = ("y_hi", "x_hi", "x_lo", "core", "z_hi", "z_lo", "y_lo")
SIZES = (2, 2, 2, 2, 16, 2, 2)
PLANE = ("core", "y_hi", "x_hi", "y_lo", "x_lo")

BLOCK = 8
HALF = 4
LANES = 128
SPARE = (3, 7)
FILLED = (0, 1, 2, 4, 5, 6)
PARTS = 4

epsilon = 1e-06
VMEM = pl.BlockSpec(memory_space=pltpu.VMEM)
SMEM = pl.BlockSpec(memory_space=pltpu.SMEM)
HBM = pl.BlockSpec(memory_space=pltpu.HBM)
PARAMS = pltpu.CompilerParams(vmem_limit_bytes=24 << 20)


def row_norm(rows):
    return jnp.sqrt(jnp.sum(rows * rows, axis=1, keepdims=True) + epsilon)


def pack(rows):
    main = rows.shape[2] - len(SPARE) * LANES
    place = lax.broadcasted_iota(jnp.int32, (rows.shape[0], BLOCK, LANES), 1)
    runs = []
    for run in range(main // LANES):
        here = rows[:, :, run * LANES : (run + 1) * LANES]
        for step, spare in enumerate(SPARE):
            if run < len(FILLED):
                at = main + step * LANES
                moved = rows[:, FILLED[run] : FILLED[run] + 1, at : at + LANES]
                here = jnp.where(place == spare, moved, here)
            else:
                here = jnp.where(place == spare, 0.0, here)
        runs.append(here)
    return jnp.concatenate(runs, axis=2)


def unpack(rows):
    place = lax.broadcasted_iota(jnp.int32, (rows.shape[0], BLOCK, LANES), 1)
    runs = []
    for run in range(rows.shape[2] // LANES):
        here = rows[:, :, run * LANES : (run + 1) * LANES]
        for spare in SPARE:
            here = jnp.where(place == spare, 0.0, here)
        runs.append(here)
    for spare in SPARE:
        tail = jnp.zeros(place.shape, rows.dtype)
        for run, filled in enumerate(FILLED):
            moved = rows[:, spare : spare + 1, run * LANES : (run + 1) * LANES]
            tail = jnp.where(place == filled, moved, tail)
        runs.append(tail)
    return jnp.concatenate(runs, axis=2)


def unpack_rows(rows):
    wide = unpack(rows.astype(jnp.float32).reshape(-1, BLOCK, rows.shape[1]))
    return wide.reshape(-1, wide.shape[2]).astype(jnp.bfloat16)


def units_kernel(
    lengths_at,
    keys_at,
    values_at,
    probe,
    projection_at,
    text,
    block,
    copies,
    projected,
    lengths,
    keys,
    values,
    projection,
    pooled,
    units,
    arrived,
):
    deep = projection.shape[0] // PARTS
    fetches = [
        pltpu.make_async_copy(source, target, arrived.at[i])
        for i, (source, target) in enumerate(
            [
                (lengths_at, lengths),
                (keys_at, keys),
                (values_at, values),
            ]
            + [
                (projection_at.at[pl.ds(part * deep, deep)], projection.at[pl.ds(part * deep, deep)])
                for part in range(PARTS)
            ]
        )
    ]
    for fetch in fetches:
        fetch.start()
    n_rows, width = keys.shape
    head = lax.broadcasted_iota(jnp.int32, (H, width), 0)
    own = lax.broadcasted_iota(jnp.int32, (H, width), 1) // HD == head
    query = jnp.where(own, probe[...].astype(jnp.float32).reshape(1, width), 0.0).astype(jnp.bfloat16)
    fetches[0].wait()
    fetches[1].wait()
    scores = lax.dot_general(
        query, keys[...], (((1,), (1,)), ((), ())), preferred_element_type=jnp.float32
    ) / math.sqrt(HD)
    row = lax.broadcasted_iota(jnp.int32, (H, n_rows), 1)
    start = jnp.int32(0)
    weights = []
    for image in range(lengths.shape[1]):
        end = start + lengths[0, image]
        member = (row >= start) & (row < end)
        masked = jnp.where(member, scores, -jnp.inf)
        terms = jnp.exp(masked - jnp.max(masked, axis=1, keepdims=True))
        weights.append((terms / jnp.sum(terms, axis=1, keepdims=True)).astype(jnp.bfloat16))
        start = end
    fetches[2].wait()
    mixed = jnp.dot(
        jnp.concatenate(weights), values[...], preferred_element_type=jnp.float32
    )
    pooled[...] = jnp.zeros_like(pooled)
    for image in range(lengths.shape[1]):
        part = mixed[image * H : (image + 1) * H]
        pooled[image : image + 1, :] = jnp.sum(jnp.where(own, part, 0.0), axis=0, keepdims=True)
    proj = jnp.zeros((2 * BLOCK, projected.shape[1]), jnp.float32)
    for part in range(PARTS):
        fetches[3 + part].wait()
        here = slice(part * deep, (part + 1) * deep)
        proj += jnp.dot(
            pooled[:, here].astype(jnp.bfloat16),
            projection[here, :],
            preferred_element_type=jnp.float32,
        )
    proj = proj[:BLOCK]
    projected[...] = proj
    units[...] = proj / row_norm(proj)
    text_wide = text[...].astype(jnp.float32)
    count = text.shape[0]
    units[HALF : HALF + count, :] = text_wide / row_norm(text_wide)
    packed = pack(units[...][None])
    block[...] = packed[0].astype(jnp.bfloat16)
    n = copies.shape[0] // BLOCK
    copies[...] = (
        jnp.broadcast_to(packed, (n,) + packed.shape[1:]).reshape(copies.shape).astype(jnp.bfloat16)
    )


def pick(groups, positions, axis):
    n_rows, lanes = groups.shape
    n = positions.shape[axis]
    high, low = groups // 64, groups % 64
    pieces = []
    for digit in (high, low):
        digit = digit.astype(jnp.float32).astype(jnp.bfloat16)
        if axis == 0:
            lane = lax.broadcasted_iota(jnp.int32, (n, lanes), 1)
            hot = jnp.where(lane == positions % lanes, 1.0, 0.0).astype(jnp.bfloat16)
            found = lax.dot_general(
                hot, digit, (((1,), (1,)), ((), ())), preferred_element_type=jnp.float32
            )
            line = lax.broadcasted_iota(jnp.int32, (n, n_rows), 1)
        else:
            lane = lax.broadcasted_iota(jnp.int32, (lanes, n), 0)
            hot = jnp.where(lane == positions % lanes, 1.0, 0.0).astype(jnp.bfloat16)
            found = jnp.dot(digit, hot, preferred_element_type=jnp.float32)
            line = lax.broadcasted_iota(jnp.int32, (n_rows, n), 0)
        kept = jnp.where(line == positions // lanes, found, 0.0)
        pieces.append(jnp.sum(kept, axis=1 - axis, keepdims=True))
    return pieces[0] * 64.0 + pieces[1]


def device(place, sizes):
    number = 0
    for axis in AXES:
        number = number * sizes[axis] + place[axis]
    return number


def tile_kernel(count, plane, *refs):
    *lines, groups, scale, bias, parts = refs
    line = jnp.concatenate([unpack_rows(rows[...]) for rows in lines])
    sizes = dict((axis, lax.axis_size(axis)) for axis in AXES)
    place = dict((axis, lax.axis_index(axis)) for axis in AXES)
    at = lax.broadcasted_iota(jnp.int32, (plane.shape[0], 1), 0)
    member, slot = at // BLOCK, jnp.minimum(at % HALF, count - 1)
    there = dict(place)
    for axis in PLANE[::-1]:
        there[axis] = member % sizes[axis]
        member = member // sizes[axis]
    plane_at = device(there, sizes) * count + slot
    plane_kind = at % BLOCK // HALF
    at = lax.broadcasted_iota(jnp.int32, (1, line.shape[0]), 1)
    member, slot = at // BLOCK, jnp.minimum(at % HALF, count - 1)
    behind = place["z_lo"] - member // sizes["z_hi"] + sizes["z_lo"]
    there = dict(place, z_hi=member % sizes["z_hi"], z_lo=behind % sizes["z_lo"])
    line_at = device(there, sizes) * count + slot
    line_kind = at % BLOCK // HALF
    plane_ids = pick(groups[...], plane_at, 0)
    line_ids = pick(groups[...], line_at, 1)

    plane_rows = unpack_rows(plane[...])
    logits = (
        lax.dot_general(
            plane_rows, line, (((1,), (1,)), ((), ())), preferred_element_type=jnp.float32
        )
        * scale[0]
        + bias[0]
    )
    labels = jnp.where(plane_ids == line_ids, 1.0, -1.0)
    coeffs = -labels * jax.nn.sigmoid(-labels * logits) * scale[0]
    coeffs = jnp.where(plane_kind != line_kind, coeffs, 0.0).astype(jnp.bfloat16)
    wide = jnp.dot(coeffs, line, preferred_element_type=jnp.float32)
    packed = pack(wide.reshape(-1, BLOCK, wide.shape[1]))
    parts[...] = packed.reshape(parts.shape).astype(jnp.bfloat16)


def grads_kernel(parts, projected, projection, text, pooled_grad, text_grad, sums):
    count, width = text.shape
    total = parts[...].astype(jnp.float32).reshape(-1, BLOCK, parts.shape[1])
    total = unpack(jnp.sum(total, axis=0, keepdims=True))[0]
    sums[...] = total
    proj = projected[...]
    norm = row_norm(proj)
    u = proj / norm
    d_proj = (total - jnp.sum(total * u, axis=1, keepdims=True) * u) / norm
    d_proj = jnp.concatenate([d_proj, jnp.zeros_like(d_proj)]).astype(jnp.bfloat16)
    pooled_grad[...] = lax.dot_general(
        d_proj, projection[...], (((1,), (1,)), ((), ())), preferred_element_type=jnp.float32
    )[:count]
    text_wide = text[...].astype(jnp.float32)
    norm = row_norm(text_wide)
    v = text_wide / norm
    d_txt = sums[HALF : HALF + count, :]
    text_grad[...] = (d_txt - jnp.sum(d_txt * v, axis=1, keepdims=True) * v) / norm


def exchange(rows, axis):
    shape = (lax.axis_size(axis), -1, rows.shape[1])
    return lax.all_to_all(rows.reshape(shape), axis, 0, 0, tiled=True).reshape(rows.shape)


def shards(
    patch_keys,
    patch_values,
    lengths,
    probe_query,
    projection,
    text_embeds,
    pair_group,
    logit_scale,
    logit_bias,
):
    count, width = text_embeds.shape
    depth = patch_keys.shape[1]
    n_far = lax.axis_size("z_hi")
    n_plane = lax.axis_size(PLANE)
    narrow = width - len(SPARE) * LANES
    block, copies, projected = pl.pallas_call(
        units_kernel,
        out_shape=(
            jax.ShapeDtypeStruct((BLOCK, narrow), jnp.bfloat16),
            jax.ShapeDtypeStruct((n_far * BLOCK, narrow), jnp.bfloat16),
            jax.ShapeDtypeStruct((BLOCK, width), jnp.float32),
        ),
        in_specs=[HBM] * 3 + [VMEM, HBM, VMEM],
        out_specs=(VMEM, VMEM, VMEM),
        scratch_shapes=[
            pltpu.SMEM(lengths.shape, lengths.dtype),
            pltpu.VMEM(patch_keys.shape, patch_keys.dtype),
            pltpu.VMEM(patch_values.shape, patch_values.dtype),
            pltpu.VMEM(projection.shape, projection.dtype),
            pltpu.VMEM((2 * BLOCK, depth), jnp.float32),
            pltpu.VMEM((BLOCK, width), jnp.float32),
            pltpu.SemaphoreType.DMA((3 + PARTS,)),
        ],
        compiler_params=pltpu.CompilerParams(vmem_limit_bytes=60 << 20),
        name="units",
    )(lengths, patch_keys, patch_values, probe_query, projection, text_embeds)

    far = exchange(copies, "z_hi")
    plane = block
    for axis in PLANE[::-1]:
        plane = lax.all_gather(plane, axis, axis=0, tiled=True)
    far, plane = lax.optimization_barrier((far, plane))
    n_near = lax.axis_size("z_lo")
    lines = [far]
    for ahead in range(1, n_near):
        route = [(i, (i + ahead) % n_near) for i in range(n_near)]
        lines.append(lax.ppermute(far, "z_lo", route))
    parts = pl.pallas_call(
        lambda *refs: tile_kernel(count, *refs),
        out_shape=jax.ShapeDtypeStruct((n_plane * BLOCK, narrow), jnp.bfloat16),
        in_specs=[VMEM] * (2 + n_near) + [SMEM] * 2,
        out_specs=VMEM,
        compiler_params=PARAMS,
        name="tile",
    )(
        plane,
        *lines,
        pair_group.reshape(-1, 128),
        logit_scale,
        logit_bias,
    )
    parts = exchange(parts, PLANE)
    return pl.pallas_call(
        grads_kernel,
        out_shape=(
            jax.ShapeDtypeStruct((count, depth), jnp.float32),
            jax.ShapeDtypeStruct((count, width), jnp.float32),
        ),
        in_specs=[VMEM] * 4,
        out_specs=(VMEM, VMEM),
        scratch_shapes=[pltpu.VMEM((BLOCK, width), jnp.float32)],
        compiler_params=PARAMS,
        name="grads",
    )(parts, projected, projection, text_embeds)


def solution(mesh):
    fine = Mesh(mesh.devices.reshape(SIZES), AXES)
    rows = P(AXES, None)
    in_specs = (rows, rows, rows, P(), P(), rows, P(), P(), P())
    return jax.shard_map(
        shards, mesh=fine, in_specs=in_specs, out_specs=(rows, rows), check_vma=False
    )
```
